512 devices in a mesh: stream: 4 (over x), span: 8 (over y, core), normal: 16 (over z).
Axes of the slice: x: 4, y: 4, z: 16, core: 2. Of those that a mesh axis runs over, the one named last changes fastest.
Arguments:
- state: float32 [5, 512, 64, 512], P(None, 'normal', 'span', 'stream'), may hold values from -5 to 5
- speeds: float32 [3, 512, 64, 512], P(None, 'normal', 'span', 'stream'), may hold values from -4 to 4
- damping: float32 [512, 64, 512], P('normal', 'span', 'stream'), may hold values from 0.02 to 0.2
- source: float32 [5, 512, 64, 512], P(None, 'normal', 'span', 'stream'), may hold values from -5 to 5.5
- normal_stiff: float32 [512, 64, 512], P('normal', 'span', 'stream'), may hold values from 10 to 1000
- wide_stiff: float32 [512, 64, 512], P('normal', 'span', 'stream'), may hold values from 2 to 200
- char_rates: float32 [5], replicated, may hold values from 0.5 to 2
- left_vectors: float32 [5, 5], replicated, may hold values from -0.6 to 2.1
- right_vectors: float32 [5, 5], replicated, may hold values from -0.6 to 2.1
Outputs:
- update: float32 [5, 512, 64, 512], P(None, 'normal', 'span', 'stream')
The draws below stay inside these ranges and needn't reach their ends.
All inputs are finite; a program needn't handle non-finite values.
Results may differ from the reference program's by a relative error of at most 0.0003.
Values sent between devices are 32-bit elements; how exact they have to be, the bound alone decides.
A program may use at most 128 MiB of HBM per device.

```python
import math
import jax
import jax.numpy as jnp
from jax import lax

VARS = 5
NX = 512
NY = 64
NZ = 512


def draw_source(key, part):
    key = jax.random.fold_in(key, 11)
    rough_key, phase_key, height_key = jax.random.split(key, 3)
    heights = jnp.arange(NZ, dtype=jnp.float32)[None, :, None, None]
    phase = jax.random.uniform(phase_key, (VARS, 1, NY, NX), jnp.float32, 0.0, 6.2831853)
    amplitude = jax.random.uniform(height_key, (VARS, 1, NY, NX), jnp.float32, 0.5, 1.5)
    wave = amplitude * jnp.sin(heights * (12.566371 / NZ) + phase)
    rough = jax.random.truncated_normal(rough_key, -3.5, 3.5, (VARS, NZ, NY, NX), jnp.float32)
    return rough + wave


def draw_left_vectors(key, part):
    key = jax.random.fold_in(key, 23)
    spread_part = jax.random.uniform(key, (VARS, VARS), jnp.float32, -0.5, 0.5)
    return 1.5 * jnp.eye(VARS, dtype=jnp.float32) + spread_part


def draw_right_vectors(key, part):
    key = jax.random.fold_in(key, 37)
    spread_part = jax.random.uniform(key, (VARS, VARS), jnp.float32, -0.5, 0.5)
    return 1.5 * jnp.eye(VARS, dtype=jnp.float32) + spread_part


def levels(rng, dims, pieces, smallest, largest):
    loudness, own = 1.0, jax.random.fold_in(rng, 6)
    for position, parts in pieces:
        steps = jnp.exp(jax.random.uniform(jax.random.fold_in(own, position), (parts,), jnp.float32, smallest / len(pieces), largest / len(pieces)))
        loudness = loudness * jnp.repeat(steps, dims[position] // parts).reshape([-1 if axis == position else 1 for axis in range(len(dims))])
    return loudness


def scatter_about(key, dims, deviation, limit, cuts=(), held_as=jnp.bfloat16):
    drawn = deviation * jax.random.normal(key, dims, jnp.float32)
    if cuts:
        drawn = drawn * levels(key, dims, cuts, -0.22, 0.18)
    return jnp.clip(drawn, -limit, limit).astype(held_as)


def setup_inputs(seed: int = 0) -> dict:
    arg_keys = jax.random.split(jax.random.key(seed), 10)
    state = scatter_about(arg_keys[0], (VARS, NZ, NY, NX), 1.0, 5.0, ((1, 16), (2, 8), (3, 4)), jnp.float32)
    speeds = scatter_about(arg_keys[1], (3, NZ, NY, NX), 1.0, 4.0, ((1, 16), (2, 8), (3, 4)), jnp.float32)
    damping = jnp.clip(jnp.exp(math.log(0.2) - 2.3025851 * jax.random.uniform(arg_keys[2], (NZ, NY, NX), jnp.float32) ** levels(arg_keys[2], (NZ, NY, NX), ((0, 16), (1, 8), (2, 4)), -0.2, 0.2)), 0.02, 0.2)
    source = draw_source(jax.random.fold_in(arg_keys[9], 71), 0)
    normal_stiff = jnp.clip(jnp.exp(math.log(1000.0) - 4.6051702 * jax.random.uniform(arg_keys[4], (NZ, NY, NX), jnp.float32) ** levels(arg_keys[4], (NZ, NY, NX), ((0, 16), (1, 8), (2, 4)), -0.2, 0.2)), 10.0, 1000.0)
    wide_stiff = jnp.clip(jnp.exp(math.log(200.0) - 4.6051702 * jax.random.uniform(arg_keys[5], (NZ, NY, NX), jnp.float32) ** levels(arg_keys[5], (NZ, NY, NX), ((0, 16), (1, 8), (2, 4)), -0.2, 0.2)), 2.0, 200.0)
    char_rates = jnp.clip(jnp.exp(jax.random.uniform(arg_keys[6], (VARS,), jnp.float32, math.log(0.5), math.log(2.0))), 0.5, 2.0)
    left_vectors = draw_left_vectors(jax.random.fold_in(arg_keys[9], 71), 0)
    right_vectors = draw_right_vectors(jax.random.fold_in(arg_keys[9], 71), 0)
    return dict(state=state, speeds=speeds, damping=damping, source=source, normal_stiff=normal_stiff, wide_stiff=wide_stiff, char_rates=char_rates, left_vectors=left_vectors, right_vectors=right_vectors)


def shifted(array, spatial, offset):
    picks = [slice(2, -2), slice(2, -2), slice(2, -2)]
    length = array.shape[array.ndim - 3 + spatial]
    picks[spatial] = slice(2 + offset, length - 2 + offset)
    leading = tuple(slice(None) for _ in range(array.ndim - 3))
    return array[leading + tuple(picks)]


def stencil_residual(state_ext, speed_ext, damping):
    flux_total = 0.0
    smooth_total = 0.0
    for spatial in range(3):
        flux = speed_ext[spatial][None] * state_ext
        flux_total = flux_total + (-shifted(flux, spatial, 2) + 8.0 * shifted(flux, spatial, 1) - 8.0 * shifted(flux, spatial, -1) + shifted(flux, spatial, -2)) / 12.0
        smooth_total = smooth_total + shifted(state_ext, spatial, 2) - 4.0 * shifted(state_ext, spatial, 1) + 6.0 * shifted(state_ext, spatial, 0) - 4.0 * shifted(state_ext, spatial, -1) + shifted(state_ext, spatial, -2)
    return -flux_total - damping[None] * smooth_total


def banded_solve(couple_near, couple_far, right):
    def forward(carried, inputs):
        near_prev, far_prev, value_prev, near_back, far_back, value_back = carried
        near, far, rhs_row = inputs
        lower_far = -far
        lower_near = -near - lower_far * near_back
        diagonal = 1.0 + 2.0 * near + 2.0 * far - lower_far * far_back
        rhs_row = rhs_row - lower_far * value_back
        diagonal = diagonal - lower_near * near_prev
        upper_near = -near - lower_near * far_prev
        rhs_row = rhs_row - lower_near * value_prev
        new_near = upper_near / diagonal
        new_far = -far / diagonal
        new_value = rhs_row / diagonal
        return (new_near, new_far, new_value, near_prev, far_prev, value_prev), (new_near, new_far, new_value)

    coef_zero = jnp.zeros_like(couple_near[0])
    value_zero = jnp.zeros_like(right[0])
    start = (coef_zero, coef_zero, value_zero, coef_zero, coef_zero, value_zero)
    _, (nears, fars, values) = lax.scan(forward, start, (couple_near, couple_far, right))

    def backward(carried, inputs):
        next_one, next_two = carried
        near, far, value_row = inputs
        solved = value_row - near * next_one - far * next_two
        return (solved, next_one), solved

    _, solution = lax.scan(backward, (value_zero, value_zero), (nears, fars, values), reverse=True)
    return solution


def reference(state, speeds, damping, source, normal_stiff, wide_stiff, char_rates, left_vectors, right_vectors):
    speed_ext = jnp.pad(speeds, ((0, 0), (2, 2), (2, 2), (2, 2)))

    def one_variable(variable):
        return stencil_residual(jnp.pad(variable, 2)[None], speed_ext, damping)[0]

    right_hand = lax.map(one_variable, state) + source
    characteristic = jnp.einsum("cv,vzyx->czyx", left_vectors, right_hand, precision=lax.Precision.HIGHEST)

    def one_field(packed):
        rate, field = packed
        return banded_solve(rate * normal_stiff, rate * wide_stiff, field)

    solved = lax.map(one_field, (char_rates, characteristic))
    return jnp.einsum("vc,czyx->vzyx", right_vectors, solved, precision=lax.Precision.HIGHEST)
```

```python
import functools

import jax
import jax.numpy as jnp
from jax import lax
from jax.experimental import pallas as pl
from jax.experimental.pallas import tpu as pltpu
from jax.sharding import PartitionSpec as P

MESH = pl.DeviceIdType.MESH
NV = 5
F32 = jnp.float32


def kernel(
    nstream, nspan, nnorm,
    state, speeds, damping, source, nstiff, wstiff, rates, left, right,
    out,
    st, spz, spy, spx, dmp, src, ns, ws,
    yh, xpack, xh_l, xh_r,
    inv_s, m_s, far_s, near_s, a_s, b_s, v_s,
    ab_send, ab_recv, de, pq, rc,
    w_send, w_recv, vrow, rr_send, rr, tri, sp, xsep, o_s, consts,
    load_sem, out_sem, halo_send, halo_recv, nb_send, nb_recv,
    c_send, c_recv, r_send, r_recv, s_send, s_recv,
):
    K = nstiff.shape[0]
    sx = lax.axis_index("stream")
    sy = lax.axis_index("span")
    sz = lax.axis_index("normal")
    x_next, x_prev = lax.rem(sx + 1, nstream), lax.rem(sx + nstream - 1, nstream)
    y_next, y_prev = lax.rem(sy + 1, nspan), lax.rem(sy + nspan - 1, nspan)
    z_next, z_prev = lax.rem(sz + 1, nnorm), lax.rem(sz + nnorm - 1, nnorm)
    at_xn, at_xp = (x_next, sy, sz), (x_prev, sy, sz)
    at_yn, at_yp = (sx, y_next, sz), (sx, y_prev, sz)
    at_zn, at_zp = (sx, sy, z_next), (sx, sy, z_prev)

    loads = [
        (nstiff, ns), (wstiff, ws), (state, st.at[:, 2:K + 2]), (speeds.at[2], spx), (speeds.at[0], spz.at[2:K + 2]),
        (speeds.at[1], spy), (damping, dmp), (source, src),
    ]
    load = [pltpu.make_async_copy(a, b, load_sem.at[i]) for i, (a, b) in enumerate(loads)]
    for c in load:
        c.start()

    barrier = pltpu.get_barrier_semaphore()
    for there in (at_xn, at_xp, at_yn, at_yp):
        pl.semaphore_signal(barrier, inc=1, device_id=there, device_id_type=MESH)

    @pl.loop(1, nnorm)
    def _(d):
        pl.semaphore_signal(barrier, inc=1, device_id=(sx, sy, lax.rem(sz + d, nnorm)), device_id_type=MESH)

    pl.semaphore_wait(barrier, nnorm + 3)

    def remote(a, b, s, r, there):
        return pltpu.make_async_remote_copy(
            src_ref=a, dst_ref=b, send_sem=s, recv_sem=r, device_id=there, device_id_type=MESH
        )

    halo_list = [
        (state.at[:, :, 6:8, :], yh.at[0:NV, :, 6:8, :], at_yn),
        (state.at[:, :, 0:2, :], yh.at[0:NV, :, 0:2, :], at_yp),
        (speeds.at[1, :, 6:8, :], yh.at[NV, :, 6:8, :], at_yn),
        (speeds.at[1, :, 0:2, :], yh.at[NV, :, 0:2, :], at_yp),
        (state.at[:, K - 2:K], st.at[:, 0:2], at_zn),
        (state.at[:, 0:2], st.at[:, K + 2:K + 4], at_zp),
        (speeds.at[0, K - 2:K], spz.at[0:2], at_zn),
        (speeds.at[0, 0:2], spz.at[K + 2:K + 4], at_zp),
    ]
    halos = [
        remote(a, b, halo_send.at[i], halo_recv.at[i], there) for i, (a, b, there) in enumerate(halo_list)
    ]
    for c in halos:
        c.start()

    lane = lax.broadcasted_iota(jnp.int32, (8, 128), 1)
    row = lax.broadcasted_iota(jnp.int32, (8, 128), 0)

    load[2].wait()
    load[3].wait()
    quad = lane // 4

    def pack(k, acc):
        here = quad == k
        tiles = [st[v, k + 2] for v in range(NV)] + [spx[k]]
        return tuple(jnp.where(here, pltpu.roll(t, 4 * k + 2, 1), a) for t, a in zip(tiles, acc))

    packed = lax.fori_loop(0, K, pack, tuple(spx[0] for _ in range(NV + 1)))
    for i, p in enumerate(packed):
        xpack[i] = p
    xcopies = [
        remote(xpack, xh_l, halo_send.at[8], halo_recv.at[8], at_xn),
        remote(xpack, xh_r, halo_send.at[9], halo_recv.at[9], at_xp),
    ]
    for c in xcopies:
        c.start()

    load[0].wait()
    load[1].wait()
    consts[0] = jnp.zeros((8, 128), F32)
    consts[1] = jnp.ones((8, 128), F32)
    zero, one = consts[0], consts[1]

    def factor(k, carry):
        g0, h0 = ns[k], ws[k]
        new = []
        for c in range(NV):
            near_p, far_p, a_p, b_p, near_b, far_b, a_b, b_b = carry[c]
            rate = rates[c]
            g, h = rate * g0, rate * h0
            low = h * near_b - g
            diag = (1.0 + 2.0 * (g + h)) + h * far_b - low * near_p
            inv = 1.0 / diag
            m = low * inv
            hi = h * inv
            near = (-g - low * far_p) * inv
            a = hi * a_b - m * a_p
            b = hi * b_b - m * b_p
            inv_s[c, k] = inv
            m_s[c, k] = m
            far_s[c, k] = hi
            near_s[c, k] = near
            a_s[c, k] = a
            b_s[c, k] = b
            new.append((near, -hi, a, b, near_p, far_p, a_p, b_p))
        return tuple(new)

    lax.fori_loop(0, K, factor, tuple((zero, zero, zero, one, zero, zero, one, zero) for _ in range(NV)))

    def spikes(i, carry):
        k = K - 3 - i
        new = []
        for c in range(NV):
            near, hi = near_s[c, k], far_s[c, k]
            ones = carry[c][0:4]
            twos = carry[c][4:8]
            base = (a_s[c, k], b_s[c, k], None, None)
            fresh = []
            for o, t, q in zip(ones, twos, base):
                r = hi * t - near * o
                fresh.append(r if q is None else r + q)
            new.append(tuple(fresh) + ones)
        return tuple(new)

    start = (zero, zero, one, zero, zero, zero, zero, one)
    done = lax.fori_loop(0, K - 2, spikes, tuple(start for _ in range(NV)))
    for c in range(NV):
        r0, r1 = done[c][0:4], done[c][4:8]
        for e, val in enumerate((r0[0], r0[1], r1[0], r1[1], r0[2], r0[3], r1[2], r1[3])):
            ab_send[e, c] = val
    ab_copy = remote(ab_send, ab_recv, nb_send.at[0], nb_recv.at[0], at_zp)
    ab_copy.start()

    is_last = sz == nnorm - 1
    ab_copy.wait_recv()

    @pl.when(is_last)
    def _():
        @pl.loop(0, 8)
        def _(e):
            for c in range(NV):
                ab_recv[e, c] = zero

    @pl.loop(0, NV)
    def _(c):
        n30, n31, h30, h31 = near_s[c, K - 2], near_s[c, K - 1], far_s[c, K - 2], far_s[c, K - 1]
        a30, a31, b30, b31 = a_s[c, K - 2], a_s[c, K - 1], b_s[c, K - 2], b_s[c, K - 1]
        n00, n01, n10, n11 = n30 * n31 + h30, -n30 * h31, -n31, h31
        s00, s01, s10, s11 = a30 - n30 * a31, b30 - n30 * b31, a31, b31
        A00, A01, A10, A11 = ab_recv[0, c], ab_recv[1, c], ab_recv[2, c], ab_recv[3, c]
        B00, B01, B10, B11 = ab_recv[4, c], ab_recv[5, c], ab_recv[6, c], ab_recv[7, c]
        m00 = 1.0 - (n00 * A00 + n01 * A10)
        m01 = -(n00 * A01 + n01 * A11)
        m10 = -(n10 * A00 + n11 * A10)
        m11 = 1.0 - (n10 * A01 + n11 * A11)
        det = 1.0 / (m00 * m11 - m01 * m10)
        d00, d01, d10, d11 = m11 * det, -m01 * det, -m10 * det, m00 * det
        e00, e01 = d00 * n00 + d01 * n10, d00 * n01 + d01 * n11
        e10, e11 = d10 * n00 + d11 * n10, d10 * n01 + d11 * n11
        for i, val in enumerate((d00, d01, d10, d11, e00, e01, e10, e11)):
            de[i, c] = val
        pq[0, c] = d00 * s00 + d01 * s10
        pq[1, c] = d00 * s01 + d01 * s11
        pq[2, c] = d10 * s00 + d11 * s10
        pq[3, c] = d10 * s01 + d11 * s11
        pq[4, c] = e00 * B00 + e01 * B10
        pq[5, c] = e00 * B01 + e01 * B11
        pq[6, c] = e10 * B00 + e11 * B10
        pq[7, c] = e10 * B01 + e11 * B11

    def scatter(rows, land, s, r, t):
        return remote(
            rows.at[:, pl.ds(2 * (t // 8), 3), lax.rem(t, 8), :], land.at[sz, :, 0:3, :],
            s.at[t], r.at[sz], (sx, sy, t),
        )

    def scatter_in(rows, land, s, r, t):
        return remote(
            rows.at[:, pl.ds(0, 3), 0, :], land.at[t, :, 0:3, :],
            s.at[t], r.at[t], (sx, sy, t),
        )

    def scatter_own(rows, land, r):
        return pltpu.make_async_copy(
            rows.at[:, pl.ds(2 * (sz // 8), 3), lax.rem(sz, 8), :], land.at[sz, :, 0:3, :], r.at[sz]
        )

    def send_all(rows, land, s, r):
        @pl.loop(1, nnorm)
        def _(d):
            scatter(rows, land, s, r, lax.rem(sz + d, nnorm)).start()

        scatter_own(rows, land, r).start()

    def recv_all(rows, land, s, r):
        @pl.loop(1, nnorm)
        def _(d):
            scatter_in(rows, land, s, r, lax.rem(sz + d, nnorm)).wait_recv()

        scatter_own(rows, land, r).wait()

    def drain_all(rows, land, s, r):
        @pl.loop(1, nnorm)
        def _(d):
            scatter(rows, land, s, r, lax.rem(sz + d, nnorm)).wait_send()

    send_all(pq, rc, c_send, c_recv)

    for c in load[4:8]:
        c.wait()
    for c in halos:
        c.wait_recv()
    for c in xcopies:
        c.wait_recv()

    @pl.when(sz == 0)
    def _():
        for v in range(NV):
            st[v, 0] = zero
            st[v, 1] = zero

    @pl.when(is_last)
    def _():
        for v in range(NV):
            st[v, K + 2] = zero
            st[v, K + 3] = zero

    take_left = lax.rem(lane, 4) < 2
    for i in range(NV + 1):
        xpack_h = jnp.where(take_left, xh_l[i], xh_r[i])
        xh_l[i] = xpack_h

    def gate(inside, ok):
        return jnp.where(inside, one, jnp.where(ok, 1.0, 0.0).astype(F32) * one)

    has_xn, has_xp = sx < nstream - 1, sx > 0
    has_yn, has_yp = sy < nspan - 1, sy > 0
    gx_p1, gx_p2 = gate(lane < 127, has_xn), gate(lane < 126, has_xn)
    gx_m1, gx_m2 = gate(lane > 0, has_xp), gate(lane > 1, has_xp)
    gy_p1, gy_p2 = gate(row < 7, has_yn), gate(row < 6, has_yn)
    gy_m1, gy_m2 = gate(row > 0, has_yp), gate(row > 1, has_yp)

    def around(t, h, index, size, axis):
        return (
            pltpu.roll(jnp.where(index < 1, h, t), size - 1, axis),
            pltpu.roll(jnp.where(index < 2, h, t), size - 2, axis),
            pltpu.roll(jnp.where(index >= size - 1, h, t), 1, axis),
            pltpu.roll(jnp.where(index >= size - 2, h, t), 2, axis),
        )

    C1, C2 = 2.0 / 3.0, 1.0 / 12.0

    def level(k, carry):
        d = dmp[k]
        d4 = 4.0 * d
        shift = 126 - 4 * k
        hx = [pltpu.roll(xh_l[i], shift, 1) for i in range(NV + 1)]
        xp1, xp2, xm1, xm2 = around(spx[k], hx[NV], lane, 128, 1)
        yp1, yp2, ym1, ym2 = around(spy[k], yh[NV, k], row, 8, 0)
        zm2, zm1, zp1, zp2 = spz[k], spz[k + 1], spz[k + 3], spz[k + 4]
        wx = ((d4 - C1 * xp1) * gx_p1, (C2 * xp2 - d) * gx_p2, (d4 + C1 * xm1) * gx_m1, (-d - C2 * xm2) * gx_m2)
        wy = ((d4 - C1 * yp1) * gy_p1, (C2 * yp2 - d) * gy_p2, (d4 + C1 * ym1) * gy_m1, (-d - C2 * ym2) * gy_m2)
        wz = (d4 - C1 * zp1, C2 * zp2 - d, d4 + C1 * zm1, -d - C2 * zm2)
        wc = -18.0 * d
        rhs = []
        for v in range(NV):
            t = st[v, k + 2]
            acc = src[v, k] + wc * t
            zs = (st[v, k + 3], st[v, k + 4], st[v, k + 1], st[v, k])
            accz = wz[0] * zs[0] + wz[1] * zs[1] + wz[2] * zs[2] + wz[3] * zs[3]
            xs = around(t, hx[v], lane, 128, 1)
            accx = wx[0] * xs[0] + wx[1] * xs[1] + wx[2] * xs[2] + wx[3] * xs[3]
            ys = around(t, yh[v, k], row, 8, 0)
            accy = wy[0] * ys[0] + wy[1] * ys[1] + wy[2] * ys[2] + wy[3] * ys[3]
            rhs.append((acc + accz) + (accx + accy))
        new = []
        for c in range(NV):
            f = left[c, 0] * rhs[0]
            for v in range(1, NV):
                f = f + left[c, v] * rhs[v]
            one_back, two_back = carry[c]
            val = f * inv_s[c, k] + far_s[c, k] * two_back - m_s[c, k] * one_back
            v_s[c, k] = val
            new.append((val, one_back))
        return tuple(new)

    ends = lax.fori_loop(0, K, level, tuple((zero, zero) for _ in range(NV)))

    def back(i, carry):
        k = K - 3 - i
        return tuple(
            (v_s[c, k] + far_s[c, k] * carry[c][1] - near_s[c, k] * carry[c][0], carry[c][0]) for c in range(NV)
        )

    firsts = lax.fori_loop(0, K - 2, back, tuple((zero, zero) for _ in range(NV)))
    for c in range(NV):
        w_send[0, c] = firsts[c][0]
        w_send[1, c] = firsts[c][1]
        v31, v30 = ends[c]
        vrow[0, c] = v30 - near_s[c, K - 2] * v31
        vrow[1, c] = v31
    w_copy = remote(w_send, w_recv, nb_send.at[1], nb_recv.at[1], at_zp)
    w_copy.start()

    recv_all(pq, rc, c_send, c_recv)

    def block_factor(j, carry):
        t00, t01, t10, t11 = carry
        p00, p01, p10, p11, q00, q01, q10, q11 = [rc[j, e] for e in range(8)]
        m00 = 1.0 - (p00 * t00 + p01 * t10)
        m01 = -(p00 * t01 + p01 * t11)
        m10 = -(p10 * t00 + p11 * t10)
        m11 = 1.0 - (p10 * t01 + p11 * t11)
        det = 1.0 / (m00 * m11 - m01 * m10)
        d00, d01, d10, d11 = m11 * det, -m01 * det, -m10 * det, m00 * det
        t00, t01 = d00 * q00 + d01 * q10, d00 * q01 + d01 * q11
        t10, t11 = d10 * q00 + d11 * q10, d10 * q01 + d11 * q11
        vals = (
            d00, d01, d10, d11,
            d00 * p00 + d01 * p10, d00 * p01 + d01 * p11, d10 * p00 + d11 * p10, d10 * p01 + d11 * p11,
            t00, t01, t10, t11,
        )
        for i, val in enumerate(vals):
            tri[j, i] = val
        return (t00, t01, t10, t11)

    lax.fori_loop(0, nnorm, block_factor, (zero, zero, zero, zero))

    w_copy.wait_recv()

    @pl.when(is_last)
    def _():
        for c in range(NV):
            w_recv[0, c] = zero
            w_recv[1, c] = zero

    for c in range(NV):
        v0, v1, w0, w1 = vrow[0, c], vrow[1, c], w_recv[0, c], w_recv[1, c]
        rr_send[0, c] = (de[0, c] * v0 + de[1, c] * v1) + (de[4, c] * w0 + de[5, c] * w1)
        rr_send[1, c] = (de[2, c] * v0 + de[3, c] * v1) + (de[6, c] * w0 + de[7, c] * w1)
    send_all(rr_send, rr, r_send, r_recv)
    recv_all(rr_send, rr, r_send, r_recv)

    def block_forward(j, carry):
        z0, z1 = carry
        r0, r1 = rr[j, 0], rr[j, 1]
        n0 = (tri[j, 0] * r0 + tri[j, 1] * r1) + (tri[j, 4] * z0 + tri[j, 5] * z1)
        n1 = (tri[j, 2] * r0 + tri[j, 3] * r1) + (tri[j, 6] * z0 + tri[j, 7] * z1)
        rr[j, 0] = n0
        rr[j, 1] = n1
        return (n0, n1)

    lax.fori_loop(0, nnorm, block_forward, (zero, zero))

    def block_back(i, carry):
        j = nnorm - 1 - i
        s0, s1 = carry
        n0 = rr[j, 0] + (tri[j, 8] * s0 + tri[j, 9] * s1)
        n1 = rr[j, 1] + (tri[j, 10] * s0 + tri[j, 11] * s1)
        sp[j + 1, 0] = n0
        sp[j + 1, 1] = n1
        return (n0, n1)

    lax.fori_loop(0, nnorm, block_back, (zero, zero))
    sp[0, 0] = zero
    sp[0, 1] = zero

    def home(t):
        return remote(
            sp.at[pl.ds(t, 2), :, 0:3, :], xsep.at[:, :, pl.ds(3 * (sz // 8), 3), lax.rem(sz, 8), :],
            s_send.at[t], s_recv.at[sz], (sx, sy, t),
        )

    def home_in(t):
        return remote(
            sp.at[pl.ds(0, 2), :, 0:3, :], xsep.at[:, :, pl.ds(3 * (t // 8), 3), lax.rem(t, 8), :],
            s_send.at[t], s_recv.at[t], (sx, sy, t),
        )

    home_own = pltpu.make_async_copy(
        sp.at[pl.ds(sz, 2), :, 0:3, :], xsep.at[:, :, pl.ds(3 * (sz // 8), 3), lax.rem(sz, 8), :], s_recv.at[sz]
    )

    @pl.loop(1, nnorm)
    def _(d):
        home(lax.rem(sz + d, nnorm)).start()

    home_own.start()

    @pl.loop(1, nnorm)
    def _(d):
        home_in(lax.rem(sz + d, nnorm)).wait_recv()

    home_own.wait()

    slot = (0, 1, 2, 4, 5)
    pre = [(xsep[0, 0, slot[c]], xsep[0, 1, slot[c]]) for c in range(NV)]
    own_s = [(xsep[1, 0, slot[c]], xsep[1, 1, slot[c]]) for c in range(NV)]

    def emit(k, xs):
        for v in range(NV):
            u = right[v, 0] * xs[0]
            for c in range(1, NV):
                u = u + right[v, c] * xs[c]
            o_s[v, k] = u

    emit(K - 1, [s[1] for s in own_s])
    emit(K - 2, [s[0] for s in own_s])

    def final(i, carry):
        k = K - 3 - i
        new = []
        for c in range(NV):
            known = v_s[c, k] + (a_s[c, k] * xsep[0, 0, slot[c]] + b_s[c, k] * xsep[0, 1, slot[c]])
            val = known + far_s[c, k] * carry[c][1] - near_s[c, k] * carry[c][0]
            new.append((val, carry[c][0]))
        emit(k, [n[0] for n in new])
        return tuple(new)

    lax.fori_loop(0, K - 2, final, tuple(own_s))
    put = pltpu.make_async_copy(o_s, out, out_sem)
    put.start()

    for c in halos:
        c.wait_send()
    for c in xcopies:
        c.wait_send()
    ab_copy.wait_send()
    w_copy.wait_send()
    drain_all(pq, rc, c_send, c_recv)
    drain_all(rr_send, rr, r_send, r_recv)

    @pl.loop(1, nnorm)
    def _(d):
        home(lax.rem(sz + d, nnorm)).wait_send()

    put.wait()


def solution(mesh):
    nstream, nspan, nnorm = mesh.shape["stream"], mesh.shape["span"], mesh.shape["normal"]

    def step(state, speeds, damping, source, normal_stiff, wide_stiff, char_rates, left_vectors, right_vectors):
        K = damping.shape[0]
        T = damping.shape[1:]
        vm = lambda *s: pltpu.VMEM(s + T, F32)
        dma = lambda n: pltpu.SemaphoreType.DMA((n,))
        hbm = pl.BlockSpec(memory_space=pltpu.HBM)
        smem = pl.BlockSpec(memory_space=pltpu.SMEM)
        per = lambda: vm(NV, K)
        return pl.pallas_call(
            functools.partial(kernel, nstream, nspan, nnorm),
            out_shape=jax.ShapeDtypeStruct(state.shape, F32),
            in_specs=[hbm] * 6 + [smem] * 3,
            out_specs=hbm,
            scratch_shapes=[
                vm(NV, K + 4), vm(K + 4), vm(K), vm(K), vm(K), vm(NV, K), vm(K), vm(K),
                vm(NV + 1, K), vm(NV + 1), vm(NV + 1), vm(NV + 1),
                per(), per(), per(), per(), per(), per(), per(),
                vm(8, NV), vm(8, NV), vm(8, NV), vm(8, NV), vm(nnorm, 8),
                vm(2, NV), vm(2, NV), vm(2, NV), vm(2, NV), vm(nnorm, 2), vm(nnorm, 12), vm(nnorm + 1, 2),
                vm(2, 2, 6), vm(NV, K), vm(2),
                dma(8), pltpu.SemaphoreType.DMA, dma(10), dma(10), dma(2), dma(2),
                dma(nnorm), dma(nnorm), dma(nnorm), dma(nnorm), dma(nnorm), dma(nnorm),
            ],
            compiler_params=pltpu.CompilerParams(
                collective_id=0, has_side_effects=True, vmem_limit_bytes=32 * 1024 * 1024
            ),
            cost_estimate=pl.CostEstimate(flops=20_000_000, bytes_accessed=2_900_000, transcendentals=0),
        )(state, speeds, damping, source, normal_stiff, wide_stiff, char_rates, left_vectors, right_vectors)

    fields = P(None, "normal", "span", "stream")
    cells = P("normal", "span", "stream")
    return jax.shard_map(
        step, mesh=mesh, in_specs=(fields, fields, cells, fields, cells, cells, P(), P(), P()),
        out_specs=fields, check_vma=False,
    )
```

```python
import functools

import jax
import jax.numpy as jnp
from jax import lax
from jax.experimental import pallas as pl
from jax.experimental.pallas import tpu as pltpu
from jax.sharding import PartitionSpec as P

MESH = pl.DeviceIdType.MESH
NV = 5
F32 = jnp.float32


def kernel(
    nstream, nspan, nnorm,
    state, speeds, damping, source, nstiff, wstiff, rates_in, left_in, right_in,
    out,
    st, spz, spy, spx, dmp, src, ns, ws,
    yh, xpack, xh_l, xh_r,
    inv_s, m_s, far_s, near_s, a_s, b_s, v_s,
    ab_send, ab_recv, de, pq, rc,
    w_send, w_recv, vrow, rr_send, rr, tri, sp, xsep, o_s, consts, rates, left, right,
    load_sem, out_sem, halo_send, halo_recv, nb_send, nb_recv,
    c_send, c_recv, r_send, r_recv, s_send, s_recv,
):
    K = nstiff.shape[0]
    sx = lax.axis_index("stream")
    sy = lax.axis_index("span")
    sz = lax.axis_index("normal")
    x_next, x_prev = lax.rem(sx + 1, nstream), lax.rem(sx + nstream - 1, nstream)
    y_next, y_prev = lax.rem(sy + 1, nspan), lax.rem(sy + nspan - 1, nspan)
    z_next, z_prev = lax.rem(sz + 1, nnorm), lax.rem(sz + nnorm - 1, nnorm)
    at_xn, at_xp = (x_next, sy, sz), (x_prev, sy, sz)
    at_yn, at_yp = (sx, y_next, sz), (sx, y_prev, sz)
    at_zn, at_zp = (sx, sy, z_next), (sx, sy, z_prev)

    loads = [
        (rates_in, rates), (nstiff, ns), (wstiff, ws), (state, st.at[:, 2:K + 2]), (speeds.at[2], spx), (speeds.at[0], spz.at[2:K + 2]),
        (speeds.at[1], spy), (damping, dmp), (source, src), (left_in, left), (right_in, right),
    ]
    load = [pltpu.make_async_copy(a, b, load_sem.at[i]) for i, (a, b) in enumerate(loads)]
    for c in load:
        c.start()

    barrier = pltpu.get_barrier_semaphore()
    for there in (at_xn, at_xp, at_yn, at_yp):
        pl.semaphore_signal(barrier, inc=1, device_id=there, device_id_type=MESH)

    @pl.loop(1, nnorm)
    def _(d):
        pl.semaphore_signal(barrier, inc=1, device_id=(sx, sy, lax.rem(sz + d, nnorm)), device_id_type=MESH)

    def remote(a, b, s, r, there):
        return pltpu.make_async_remote_copy(
            src_ref=a, dst_ref=b, send_sem=s, recv_sem=r, device_id=there, device_id_type=MESH
        )

    lane = lax.broadcasted_iota(jnp.int32, (8, 128), 1)
    row = lax.broadcasted_iota(jnp.int32, (8, 128), 0)

    load[0].wait()
    load[1].wait()
    load[2].wait()
    consts[0] = jnp.zeros((8, 128), F32)
    consts[1] = jnp.ones((8, 128), F32)
    zero, one = consts[0], consts[1]

    def factor(k, carry):
        g0, h0 = ns[k], ws[k]
        new = []
        for c in range(NV):
            near_p, far_p, a_p, b_p, near_b, far_b, a_b, b_b = carry[c]
            rate = rates[c]
            g, h = rate * g0, rate * h0
            low = h * near_b - g
            diag = (1.0 + 2.0 * (g + h)) + h * far_b - low * near_p
            inv = 1.0 / diag
            m = low * inv
            hi = h * inv
            near = (-g - low * far_p) * inv
            a = hi * a_b - m * a_p
            b = hi * b_b - m * b_p
            inv_s[c, k] = inv
            m_s[c, k] = m
            far_s[c, k] = hi
            near_s[c, k] = near
            a_s[c, k] = a
            b_s[c, k] = b
            new.append((near, -hi, a, b, near_p, far_p, a_p, b_p))
        return tuple(new)

    lax.fori_loop(0, K, factor, tuple((zero, zero, zero, one, zero, zero, one, zero) for _ in range(NV)))

    def spikes(i, carry):
        k = K - 3 - i
        new = []
        for c in range(NV):
            near, hi = near_s[c, k], far_s[c, k]
            ones = carry[c][0:4]
            twos = carry[c][4:8]
            base = (a_s[c, k], b_s[c, k], None, None)
            fresh = []
            for o, t, q in zip(ones, twos, base):
                r = hi * t - near * o
                fresh.append(r if q is None else r + q)
            new.append(tuple(fresh) + ones)
        return tuple(new)

    start = (zero, zero, one, zero, zero, zero, zero, one)
    done = lax.fori_loop(0, K - 2, spikes, tuple(start for _ in range(NV)))
    for c in range(NV):
        r0, r1 = done[c][0:4], done[c][4:8]
        for e, val in enumerate((r0[0], r0[1], r1[0], r1[1], r0[2], r0[3], r1[2], r1[3])):
            ab_send[e, c] = val
    load[3].wait()
    load[4].wait()
    quad = lane // 4

    def pack(k, acc):
        here = quad == k
        tiles = [st[v, k + 2] for v in range(NV)] + [spx[k]]
        return tuple(jnp.where(here, pltpu.roll(t, 4 * k + 2, 1), a) for t, a in zip(tiles, acc))

    packed = lax.fori_loop(0, K, pack, tuple(spx[0] for _ in range(NV + 1)))
    for i, p in enumerate(packed):
        xpack[i] = p
    pl.semaphore_wait(barrier, nnorm + 3)

    ab_copy = remote(ab_send, ab_recv, nb_send.at[0], nb_recv.at[0], at_zp)
    ab_copy.start()

    halo_list = [
        (state.at[:, :, 6:8, :], yh.at[0:NV, :, 6:8, :], at_yn),
        (state.at[:, :, 0:2, :], yh.at[0:NV, :, 0:2, :], at_yp),
        (speeds.at[1, :, 6:8, :], yh.at[NV, :, 6:8, :], at_yn),
        (speeds.at[1, :, 0:2, :], yh.at[NV, :, 0:2, :], at_yp),
        (state.at[:, K - 2:K], st.at[:, 0:2], at_zn),
        (state.at[:, 0:2], st.at[:, K + 2:K + 4], at_zp),
        (speeds.at[0, K - 2:K], spz.at[0:2], at_zn),
        (speeds.at[0, 0:2], spz.at[K + 2:K + 4], at_zp),
    ]
    halos = [
        remote(a, b, halo_send.at[i], halo_recv.at[i], there) for i, (a, b, there) in enumerate(halo_list)
    ]
    for c in halos:
        c.start()

    xcopies = [
        remote(xpack, xh_l, halo_send.at[8], halo_recv.at[8], at_xn),
        remote(xpack, xh_r, halo_send.at[9], halo_recv.at[9], at_xp),
    ]
    for c in xcopies:
        c.start()

    is_last = sz == nnorm - 1
    ab_copy.wait_recv()

    @pl.when(is_last)
    def _():
        @pl.loop(0, 8)
        def _(e):
            for c in range(NV):
                ab_recv[e, c] = zero

    @pl.loop(0, NV)
    def _(c):
        n30, n31, h30, h31 = near_s[c, K - 2], near_s[c, K - 1], far_s[c, K - 2], far_s[c, K - 1]
        a30, a31, b30, b31 = a_s[c, K - 2], a_s[c, K - 1], b_s[c, K - 2], b_s[c, K - 1]
        n00, n01, n10, n11 = n30 * n31 + h30, -n30 * h31, -n31, h31
        s00, s01, s10, s11 = a30 - n30 * a31, b30 - n30 * b31, a31, b31
        A00, A01, A10, A11 = ab_recv[0, c], ab_recv[1, c], ab_recv[2, c], ab_recv[3, c]
        B00, B01, B10, B11 = ab_recv[4, c], ab_recv[5, c], ab_recv[6, c], ab_recv[7, c]
        m00 = 1.0 - (n00 * A00 + n01 * A10)
        m01 = -(n00 * A01 + n01 * A11)
        m10 = -(n10 * A00 + n11 * A10)
        m11 = 1.0 - (n10 * A01 + n11 * A11)
        det = 1.0 / (m00 * m11 - m01 * m10)
        d00, d01, d10, d11 = m11 * det, -m01 * det, -m10 * det, m00 * det
        e00, e01 = d00 * n00 + d01 * n10, d00 * n01 + d01 * n11
        e10, e11 = d10 * n00 + d11 * n10, d10 * n01 + d11 * n11
        for i, val in enumerate((d00, d01, d10, d11, e00, e01, e10, e11)):
            de[i, c] = val
        pq[0, c] = d00 * s00 + d01 * s10
        pq[1, c] = d00 * s01 + d01 * s11
        pq[2, c] = d10 * s00 + d11 * s10
        pq[3, c] = d10 * s01 + d11 * s11
        pq[4, c] = e00 * B00 + e01 * B10
        pq[5, c] = e00 * B01 + e01 * B11
        pq[6, c] = e10 * B00 + e11 * B10
        pq[7, c] = e10 * B01 + e11 * B11

    def either(t, do):
        pl.when(t < 8)(lambda: do(0, 3))
        pl.when(t >= 8)(lambda: do(3, 2))

    def scatter(rows, land, s, r, t, first, count):
        return remote(
            rows.at[:, first:first + count, lax.rem(t, 8), :], land.at[sz, :, 0:count, :],
            s.at[t], r.at[sz], (sx, sy, t),
        )

    def scatter_in(rows, land, s, r, t, first, count):
        return remote(
            rows.at[:, first:first + count, 0, :], land.at[t, :, 0:count, :], s.at[t], r.at[t], (sx, sy, t)
        )

    def scatter_own(rows, land, r, first, count):
        return pltpu.make_async_copy(
            rows.at[:, first:first + count, lax.rem(sz, 8), :], land.at[sz, :, 0:count, :], r.at[sz]
        )

    def send_all(rows, land, s, r):
        @pl.loop(1, nnorm)
        def _(d):
            t = lax.rem(sz + d, nnorm)
            either(t, lambda first, count: scatter(rows, land, s, r, t, first, count).start())

        either(sz, lambda first, count: scatter_own(rows, land, r, first, count).start())

    def recv_all(rows, land, s, r):
        def every(first, count):
            @pl.loop(1, nnorm)
            def _(d):
                scatter_in(rows, land, s, r, lax.rem(sz + d, nnorm), first, count).wait_recv()

            scatter_own(rows, land, r, first, count).wait()

        either(sz, every)

    def drain_all(rows, land, s, r):
        @pl.loop(1, nnorm)
        def _(d):
            t = lax.rem(sz + d, nnorm)
            either(t, lambda first, count: scatter(rows, land, s, r, t, first, count).wait_send())

    send_all(pq, rc, c_send, c_recv)

    for c in load[5:10]:
        c.wait()
    for c in halos:
        c.wait_recv()
    for c in xcopies:
        c.wait_recv()

    @pl.when(sz == 0)
    def _():
        for v in range(NV):
            st[v, 0] = zero
            st[v, 1] = zero

    @pl.when(is_last)
    def _():
        for v in range(NV):
            st[v, K + 2] = zero
            st[v, K + 3] = zero

    take_left = lax.rem(lane, 4) < 2
    for i in range(NV + 1):
        xpack_h = jnp.where(take_left, xh_l[i], xh_r[i])
        xh_l[i] = xpack_h

    def gate(inside, ok):
        return jnp.where(inside, one, jnp.where(ok, 1.0, 0.0).astype(F32) * one)

    has_xn, has_xp = sx < nstream - 1, sx > 0
    has_yn, has_yp = sy < nspan - 1, sy > 0
    gx_p1, gx_p2 = gate(lane < 127, has_xn), gate(lane < 126, has_xn)
    gx_m1, gx_m2 = gate(lane > 0, has_xp), gate(lane > 1, has_xp)
    gy_p1, gy_p2 = gate(row < 7, has_yn), gate(row < 6, has_yn)
    gy_m1, gy_m2 = gate(row > 0, has_yp), gate(row > 1, has_yp)

    def around(t, h, index, size, axis):
        return (
            pltpu.roll(jnp.where(index < 1, h, t), size - 1, axis),
            pltpu.roll(jnp.where(index < 2, h, t), size - 2, axis),
            pltpu.roll(jnp.where(index >= size - 1, h, t), 1, axis),
            pltpu.roll(jnp.where(index >= size - 2, h, t), 2, axis),
        )

    C1, C2 = 2.0 / 3.0, 1.0 / 12.0

    def level(k, carry):
        d = dmp[k]
        d4 = 4.0 * d
        shift = 126 - 4 * k
        hx = [pltpu.roll(xh_l[i], shift, 1) for i in range(NV + 1)]
        xp1, xp2, xm1, xm2 = around(spx[k], hx[NV], lane, 128, 1)
        yp1, yp2, ym1, ym2 = around(spy[k], yh[NV, k], row, 8, 0)
        zm2, zm1, zp1, zp2 = spz[k], spz[k + 1], spz[k + 3], spz[k + 4]
        wx = ((d4 - C1 * xp1) * gx_p1, (C2 * xp2 - d) * gx_p2, (d4 + C1 * xm1) * gx_m1, (-d - C2 * xm2) * gx_m2)
        wy = ((d4 - C1 * yp1) * gy_p1, (C2 * yp2 - d) * gy_p2, (d4 + C1 * ym1) * gy_m1, (-d - C2 * ym2) * gy_m2)
        wz = (d4 - C1 * zp1, C2 * zp2 - d, d4 + C1 * zm1, -d - C2 * zm2)
        wc = -18.0 * d
        rhs = []
        for v in range(NV):
            t = st[v, k + 2]
            acc = src[v, k] + wc * t
            zs = (st[v, k + 3], st[v, k + 4], st[v, k + 1], st[v, k])
            accz = wz[0] * zs[0] + wz[1] * zs[1] + wz[2] * zs[2] + wz[3] * zs[3]
            xs = around(t, hx[v], lane, 128, 1)
            accx = wx[0] * xs[0] + wx[1] * xs[1] + wx[2] * xs[2] + wx[3] * xs[3]
            ys = around(t, yh[v, k], row, 8, 0)
            accy = wy[0] * ys[0] + wy[1] * ys[1] + wy[2] * ys[2] + wy[3] * ys[3]
            rhs.append((acc + accz) + (accx + accy))
        new = []
        for c in range(NV):
            f = left[c, 0] * rhs[0]
            for v in range(1, NV):
                f = f + left[c, v] * rhs[v]
            one_back, two_back = carry[c]
            val = f * inv_s[c, k] + far_s[c, k] * two_back - m_s[c, k] * one_back
            v_s[c, k] = val
            new.append((val, one_back))
        return tuple(new)

    ends = lax.fori_loop(0, K, level, tuple((zero, zero) for _ in range(NV)))

    def back(i, carry):
        k = K - 3 - i
        return tuple(
            (v_s[c, k] + far_s[c, k] * carry[c][1] - near_s[c, k] * carry[c][0], carry[c][0]) for c in range(NV)
        )

    firsts = lax.fori_loop(0, K - 2, back, tuple((zero, zero) for _ in range(NV)))
    for c in range(NV):
        w_send[0, c] = firsts[c][0]
        w_send[1, c] = firsts[c][1]
        v31, v30 = ends[c]
        vrow[0, c] = v30 - near_s[c, K - 2] * v31
        vrow[1, c] = v31
    w_copy = remote(w_send, w_recv, nb_send.at[1], nb_recv.at[1], at_zp)
    w_copy.start()

    w_copy.wait_recv()

    @pl.when(is_last)
    def _():
        for c in range(NV):
            w_recv[0, c] = zero
            w_recv[1, c] = zero

    for c in range(NV):
        v0, v1, w0, w1 = vrow[0, c], vrow[1, c], w_recv[0, c], w_recv[1, c]
        rr_send[0, c] = (de[0, c] * v0 + de[1, c] * v1) + (de[4, c] * w0 + de[5, c] * w1)
        rr_send[1, c] = (de[2, c] * v0 + de[3, c] * v1) + (de[6, c] * w0 + de[7, c] * w1)
    send_all(rr_send, rr, r_send, r_recv)

    recv_all(pq, rc, c_send, c_recv)

    def block_factor(j, carry):
        t00, t01, t10, t11 = carry
        p00, p01, p10, p11, q00, q01, q10, q11 = [rc[j, e] for e in range(8)]
        m00 = 1.0 - (p00 * t00 + p01 * t10)
        m01 = -(p00 * t01 + p01 * t11)
        m10 = -(p10 * t00 + p11 * t10)
        m11 = 1.0 - (p10 * t01 + p11 * t11)
        det = 1.0 / (m00 * m11 - m01 * m10)
        d00, d01, d10, d11 = m11 * det, -m01 * det, -m10 * det, m00 * det
        t00, t01 = d00 * q00 + d01 * q10, d00 * q01 + d01 * q11
        t10, t11 = d10 * q00 + d11 * q10, d10 * q01 + d11 * q11
        vals = (
            d00, d01, d10, d11,
            d00 * p00 + d01 * p10, d00 * p01 + d01 * p11, d10 * p00 + d11 * p10, d10 * p01 + d11 * p11,
            t00, t01, t10, t11,
        )
        for i, val in enumerate(vals):
            tri[j, i] = val
        return (t00, t01, t10, t11)

    lax.fori_loop(0, nnorm, block_factor, (zero, zero, zero, zero))

    recv_all(rr_send, rr, r_send, r_recv)

    def block_forward(j, carry):
        z0, z1 = carry
        r0, r1 = rr[j, 0], rr[j, 1]
        n0 = (tri[j, 0] * r0 + tri[j, 1] * r1) + (tri[j, 4] * z0 + tri[j, 5] * z1)
        n1 = (tri[j, 2] * r0 + tri[j, 3] * r1) + (tri[j, 6] * z0 + tri[j, 7] * z1)
        rr[j, 0] = n0
        rr[j, 1] = n1
        return (n0, n1)

    lax.fori_loop(0, nnorm, block_forward, (zero, zero))

    def block_back(i, carry):
        j = nnorm - 1 - i
        s0, s1 = carry
        n0 = rr[j, 0] + (tri[j, 8] * s0 + tri[j, 9] * s1)
        n1 = rr[j, 1] + (tri[j, 10] * s0 + tri[j, 11] * s1)
        sp[j + 1, 0] = n0
        sp[j + 1, 1] = n1
        return (n0, n1)

    lax.fori_loop(0, nnorm, block_back, (zero, zero))
    sp[0, 0] = zero
    sp[0, 1] = zero

    def home(t, first, count):
        return remote(
            sp.at[pl.ds(t, 2), :, 0:count, :], xsep.at[:, :, first:first + count, lax.rem(sz, 8), :],
            s_send.at[t], s_recv.at[sz], (sx, sy, t),
        )

    def home_in(t, first, count):
        return remote(
            sp.at[0:2, :, 0:count, :], xsep.at[:, :, first:first + count, lax.rem(t, 8), :],
            s_send.at[t], s_recv.at[t], (sx, sy, t),
        )

    def home_own(first, count):
        return pltpu.make_async_copy(
            sp.at[pl.ds(sz, 2), :, 0:count, :], xsep.at[:, :, first:first + count, lax.rem(sz, 8), :], s_recv.at[sz]
        )

    def home_all(first, count):
        @pl.loop(1, nnorm)
        def _(d):
            home(lax.rem(sz + d, nnorm), first, count).start()

        home_own(first, count).start()

    either(sz, home_all)

    @pl.loop(1, nnorm)
    def _(d):
        t = lax.rem(sz + d, nnorm)
        either(t, lambda first, count: home_in(t, first, count).wait_recv())

    either(sz, lambda first, count: home_own(first, count).wait())

    load[10].wait()
    own_s = [(xsep[1, 0, c], xsep[1, 1, c]) for c in range(NV)]

    def emit(k, xs):
        for v in range(NV):
            u = right[v, 0] * xs[0]
            for c in range(1, NV):
                u = u + right[v, c] * xs[c]
            o_s[v, k] = u

    emit(K - 1, [s[1] for s in own_s])
    emit(K - 2, [s[0] for s in own_s])

    def final(i, carry):
        k = K - 3 - i
        new = []
        for c in range(NV):
            known = v_s[c, k] + (a_s[c, k] * xsep[0, 0, c] + b_s[c, k] * xsep[0, 1, c])
            val = known + far_s[c, k] * carry[c][1] - near_s[c, k] * carry[c][0]
            new.append((val, carry[c][0]))
        emit(k, [n[0] for n in new])
        return tuple(new)

    parts = 4
    rows = K // parts
    carry, begin = tuple(own_s), 0
    puts = []
    for p in reversed(range(parts)):
        stop = K - 2 - p * rows
        carry = lax.fori_loop(begin, stop, final, carry)
        begin = stop
        put = pltpu.make_async_copy(o_s.at[:, p * rows:(p + 1) * rows], out.at[:, p * rows:(p + 1) * rows], out_sem.at[p])
        put.start()
        puts.append(put)

    for c in halos:
        c.wait_send()
    for c in xcopies:
        c.wait_send()
    ab_copy.wait_send()
    w_copy.wait_send()
    drain_all(pq, rc, c_send, c_recv)
    drain_all(rr_send, rr, r_send, r_recv)

    def home_drain(first, count):
        @pl.loop(1, nnorm)
        def _(d):
            home(lax.rem(sz + d, nnorm), first, count).wait_send()

    either(sz, home_drain)
    for put in puts:
        put.wait()


def solution(mesh):
    nstream, nspan, nnorm = mesh.shape["stream"], mesh.shape["span"], mesh.shape["normal"]

    def step(state, speeds, damping, source, normal_stiff, wide_stiff, char_rates, left_vectors, right_vectors):
        K = damping.shape[0]
        T = damping.shape[1:]
        vm = lambda *s: pltpu.VMEM(s + T, F32)
        dma = lambda n: pltpu.SemaphoreType.DMA((n,))
        hbm = pl.BlockSpec(memory_space=pltpu.HBM)
        per = lambda: vm(NV, K)
        return pl.pallas_call(
            functools.partial(kernel, nstream, nspan, nnorm),
            out_shape=jax.ShapeDtypeStruct(state.shape, F32),
            in_specs=[hbm] * 9,
            out_specs=hbm,
            scratch_shapes=[
                vm(NV, K + 4), vm(K + 4), vm(K), vm(K), vm(K), vm(NV, K), vm(K), vm(K),
                vm(NV + 1, K), vm(NV + 1), vm(NV + 1), vm(NV + 1),
                per(), per(), per(), per(), per(), per(), per(),
                vm(8, NV), vm(8, NV), vm(8, NV), vm(8, NV), vm(nnorm, 8),
                vm(2, NV), vm(2, NV), vm(2, NV), vm(2, NV), vm(nnorm, 2), vm(nnorm, 12), vm(nnorm + 1, 2),
                vm(2, 2, NV), vm(NV, K), vm(2),
                pltpu.SMEM((NV,), F32), pltpu.SMEM((NV, NV), F32), pltpu.SMEM((NV, NV), F32),
                dma(11), dma(4), dma(10), dma(10), dma(2), dma(2),
                dma(nnorm), dma(nnorm), dma(nnorm), dma(nnorm), dma(nnorm), dma(nnorm),
            ],
            compiler_params=pltpu.CompilerParams(
                collective_id=0, has_side_effects=True, vmem_limit_bytes=60 * 1024 * 1024
            ),
            cost_estimate=pl.CostEstimate(flops=20_000_000, bytes_accessed=2_900_000, transcendentals=0),
        )(state, speeds, damping, source, normal_stiff, wide_stiff, char_rates, left_vectors, right_vectors)

    fields = P(None, "normal", "span", "stream")
    cells = P("normal", "span", "stream")
    return jax.shard_map(
        step, mesh=mesh, in_specs=(fields, fields, cells, fields, cells, cells, P(), P(), P()),
        out_specs=fields, check_vma=False,
    )
```

```python
import functools

import jax
import jax.numpy as jnp
from jax import lax
from jax.experimental import pallas as pl
from jax.experimental.pallas import tpu as pltpu
from jax.sharding import PartitionSpec as P

MESH = pl.DeviceIdType.MESH
NV = 5
F32 = jnp.float32


def kernel(
    nstream, nspan, nnorm,
    state, speeds, damping, source, nstiff, wstiff, rates_in, left_in, right_in,
    out,
    st, spz, spy, spx, dmp, src, ns, ws,
    yh, xpack, xh_l, xh_r,
    inv_s, m_s, far_s, near_s, a_s, b_s, v_s,
    a_send, a_recv, n_send, n_recv, spike, de, pq, rc,
    rr_send, rr, tri, sp, xsep, consts, rates, left, right,
    load_sem, halo_send, halo_recv, nb_send, nb_recv,
    c_send, c_recv, r_send, r_recv, s_send, s_recv,
):
    K = nstiff.shape[0]
    sx = lax.axis_index("stream")
    sy = lax.axis_index("span")
    sz = lax.axis_index("normal")
    x_next, x_prev = lax.rem(sx + 1, nstream), lax.rem(sx + nstream - 1, nstream)
    y_next, y_prev = lax.rem(sy + 1, nspan), lax.rem(sy + nspan - 1, nspan)
    z_next, z_prev = lax.rem(sz + 1, nnorm), lax.rem(sz + nnorm - 1, nnorm)
    at_xn, at_xp = (x_next, sy, sz), (x_prev, sy, sz)
    at_yn, at_yp = (sx, y_next, sz), (sx, y_prev, sz)
    at_zn, at_zp = (sx, sy, z_next), (sx, sy, z_prev)

    loads = [
        (rates_in, rates), (nstiff, ns), (wstiff, ws), (state, st.at[:, 2:K + 2]), (speeds.at[2], spx), (speeds.at[0], spz.at[2:K + 2]),
        (speeds.at[1], spy), (damping, dmp), (source, src), (left_in, left), (right_in, right),
    ]
    load = [pltpu.make_async_copy(a, b, load_sem.at[i]) for i, (a, b) in enumerate(loads)]
    for c in load:
        c.start()

    barrier = pltpu.get_barrier_semaphore()
    for there in (at_xn, at_xp, at_yn, at_yp):
        pl.semaphore_signal(barrier, inc=1, device_id=there, device_id_type=MESH)

    @pl.loop(1, nnorm)
    def _(d):
        pl.semaphore_signal(barrier, inc=1, device_id=(sx, sy, lax.rem(sz + d, nnorm)), device_id_type=MESH)

    def remote(a, b, s, r, there):
        return pltpu.make_async_remote_copy(
            src_ref=a, dst_ref=b, send_sem=s, recv_sem=r, device_id=there, device_id_type=MESH
        )

    lane = lax.broadcasted_iota(jnp.int32, (8, 128), 1)
    row = lax.broadcasted_iota(jnp.int32, (8, 128), 0)

    load[0].wait()
    load[1].wait()
    load[2].wait()
    consts[0] = jnp.zeros((8, 128), F32)
    consts[1] = jnp.ones((8, 128), F32)
    zero, one = consts[0], consts[1]

    def factor(k, carry):
        g0, h0 = ns[k], ws[k]
        new = []
        for c in range(NV):
            near_p, far_p, a_p, b_p, near_b, far_b, a_b, b_b = carry[c]
            rate = rates[c]
            g, h = rate * g0, rate * h0
            low = h * near_b - g
            diag = (1.0 + 2.0 * (g + h)) + h * far_b - low * near_p
            inv = 1.0 / diag
            m = low * inv
            hi = h * inv
            near = (-g - low * far_p) * inv
            a = hi * a_b - m * a_p
            b = hi * b_b - m * b_p
            inv_s[c, k] = inv
            m_s[c, k] = m
            far_s[c, k] = hi
            near_s[c, k] = near
            a_s[c, k] = a
            b_s[c, k] = b
            new.append((near, -hi, a, b, near_p, far_p, a_p, b_p))
        return tuple(new)

    lax.fori_loop(0, K, factor, tuple((zero, zero, zero, one, zero, zero, one, zero) for _ in range(NV)))

    def spikes(i, carry):
        k = K - 3 - i
        new = []
        for c in range(NV):
            near, hi = near_s[c, k], far_s[c, k]
            ones = carry[c][0:4]
            twos = carry[c][4:8]
            base = (a_s[c, k], b_s[c, k], None, None)
            fresh = []
            for o, t, q in zip(ones, twos, base):
                r = hi * t - near * o
                fresh.append(r if q is None else r + q)
            new.append(tuple(fresh) + ones)
        return tuple(new)

    start = (zero, zero, one, zero, zero, zero, zero, one)
    done = lax.fori_loop(0, K - 2, spikes, tuple(start for _ in range(NV)))
    for c in range(NV):
        r0, r1 = done[c][0:4], done[c][4:8]
        for e, val in enumerate((r0[0], r0[1], r1[0], r1[1])):
            a_send[e, c] = val
        for e, val in enumerate((r0[2], r0[3], r1[2], r1[3])):
            spike[e, c] = val
        n30, n31, h30, h31 = near_s[c, K - 2], near_s[c, K - 1], far_s[c, K - 2], far_s[c, K - 1]
        for e, val in enumerate((n30 * n31 + h30, -n30 * h31, -n31, h31)):
            n_send[e, c] = val
    for e in range(4):
        rc[nnorm, 4 + e] = zero
    for e in range(2):
        rr[nnorm, 2 + e] = zero

    load[3].wait()
    load[4].wait()
    quad = lane // 4

    def pack(k, acc):
        here = quad == k
        tiles = [st[v, k + 2] for v in range(NV)] + [spx[k]]
        return tuple(jnp.where(here, pltpu.roll(t, 4 * k + 2, 1), a) for t, a in zip(tiles, acc))

    packed = lax.fori_loop(0, K, pack, tuple(spx[0] for _ in range(NV + 1)))
    for i, p in enumerate(packed):
        xpack[i] = p
    pl.semaphore_wait(barrier, nnorm + 3)

    halo_list = [
        (state.at[:, :, 6:8, :], yh.at[0:NV, :, 6:8, :], at_yn),
        (state.at[:, :, 0:2, :], yh.at[0:NV, :, 0:2, :], at_yp),
        (speeds.at[1, :, 6:8, :], yh.at[NV, :, 6:8, :], at_yn),
        (speeds.at[1, :, 0:2, :], yh.at[NV, :, 0:2, :], at_yp),
        (state.at[:, K - 2:K], st.at[:, 0:2], at_zn),
        (state.at[:, 0:2], st.at[:, K + 2:K + 4], at_zp),
        (speeds.at[0, K - 2:K], spz.at[0:2], at_zn),
        (speeds.at[0, 0:2], spz.at[K + 2:K + 4], at_zp),
    ]
    halos = [
        remote(a, b, halo_send.at[i], halo_recv.at[i], there) for i, (a, b, there) in enumerate(halo_list)
    ]
    for c in halos:
        c.start()

    xcopies = [
        remote(xpack, xh_l, halo_send.at[8], halo_recv.at[8], at_xn),
        remote(xpack, xh_r, halo_send.at[9], halo_recv.at[9], at_xp),
    ]
    for c in xcopies:
        c.start()

    nb = [
        remote(a_send, a_recv, nb_send.at[0], nb_recv.at[0], at_zp),
        remote(n_send, n_recv, nb_send.at[1], nb_recv.at[1], at_zn),
    ]
    for c in nb:
        c.start()
    for c in nb:
        c.wait_recv()

    is_last = sz == nnorm - 1

    @pl.when(is_last)
    def _():
        for e in range(4):
            for c in range(NV):
                a_recv[e, c] = zero

    def inverse(n, a):
        m00 = 1.0 - (n[0] * a[0] + n[1] * a[2])
        m01 = -(n[0] * a[1] + n[1] * a[3])
        m10 = -(n[2] * a[0] + n[3] * a[2])
        m11 = 1.0 - (n[2] * a[1] + n[3] * a[3])
        det = 1.0 / (m00 * m11 - m01 * m10)
        return m11 * det, -m01 * det, -m10 * det, m00 * det

    def times(p, q):
        return (
            p[0] * q[0] + p[1] * q[2], p[0] * q[1] + p[1] * q[3],
            p[2] * q[0] + p[3] * q[2], p[2] * q[1] + p[3] * q[3],
        )

    @pl.loop(0, NV)
    def _(c):
        four = lambda ref: tuple(ref[e, c] for e in range(4))
        n30, a30, a31, b30, b31 = near_s[c, K - 2], a_s[c, K - 2], a_s[c, K - 1], b_s[c, K - 2], b_s[c, K - 1]
        d = inverse(four(n_send), four(a_recv))
        p = times(d, (a30 - n30 * a31, b30 - n30 * b31, a31, b31))
        before = four(n_recv)
        e_ = times(inverse(before, four(a_send)), before)
        q = times(e_, four(spike))
        for i in range(4):
            de[i, c] = d[i]
            de[4 + i, c] = e_[i]
            pq[i, c] = p[i]
            pq[4 + i, c] = q[i]

    def either(t, do):
        pl.when(t < 8)(lambda: do(0, 3))
        pl.when(t >= 8)(lambda: do(3, 2))

    def scatter(rows, land, s, r, t, first, count):
        return remote(
            rows.at[:, first:first + count, lax.rem(t, 8), :], land.at[sz, :, 0:count, :],
            s.at[t], r.at[sz], (sx, sy, t),
        )

    def scatter_in(rows, land, s, r, t, first, count):
        return remote(
            rows.at[:, first:first + count, 0, :], land.at[t, :, 0:count, :], s.at[t], r.at[t], (sx, sy, t)
        )

    def scatter_own(rows, land, r, first, count):
        return pltpu.make_async_copy(
            rows.at[:, first:first + count, lax.rem(sz, 8), :], land.at[sz, :, 0:count, :], r.at[sz]
        )

    def peer(i):
        return lax.rem(sz + nnorm // 2 + ((i + 1) // 2) * (1 - 2 * lax.rem(i, 2)), nnorm)

    def send_all(rows, land, s, r):
        @pl.loop(0, nnorm - 1)
        def _(i):
            t = peer(i)
            either(t, lambda first, count: scatter(rows, land, s, r, t, first, count).start())

        either(sz, lambda first, count: scatter_own(rows, land, r, first, count).start())

    def recv_all(rows, land, s, r):
        def every(first, count):
            @pl.loop(1, nnorm)
            def _(d):
                scatter_in(rows, land, s, r, lax.rem(sz + d, nnorm), first, count).wait_recv()

            scatter_own(rows, land, r, first, count).wait()

        either(sz, every)

    def drain_all(rows, land, s, r):
        @pl.loop(1, nnorm)
        def _(d):
            t = lax.rem(sz + d, nnorm)
            either(t, lambda first, count: scatter(rows, land, s, r, t, first, count).wait_send())

    send_all(pq, rc, c_send, c_recv)

    for c in load[5:10]:
        c.wait()
    for c in halos:
        c.wait_recv()
    for c in xcopies:
        c.wait_recv()

    @pl.when(sz == 0)
    def _():
        for v in range(NV):
            st[v, 0] = zero
            st[v, 1] = zero

    @pl.when(is_last)
    def _():
        for v in range(NV):
            st[v, K + 2] = zero
            st[v, K + 3] = zero

    take_left = lax.rem(lane, 4) < 2
    for i in range(NV + 1):
        xpack_h = jnp.where(take_left, xh_l[i], xh_r[i])
        xh_l[i] = xpack_h

    def gate(inside, ok):
        return jnp.where(inside, one, jnp.where(ok, 1.0, 0.0).astype(F32) * one)

    has_xn, has_xp = sx < nstream - 1, sx > 0
    has_yn, has_yp = sy < nspan - 1, sy > 0
    gx_p1, gx_p2 = gate(lane < 127, has_xn), gate(lane < 126, has_xn)
    gx_m1, gx_m2 = gate(lane > 0, has_xp), gate(lane > 1, has_xp)
    gy_p1, gy_p2 = gate(row < 7, has_yn), gate(row < 6, has_yn)
    gy_m1, gy_m2 = gate(row > 0, has_yp), gate(row > 1, has_yp)

    def around(t, h, index, size, axis):
        return (
            pltpu.roll(jnp.where(index < 1, h, t), size - 1, axis),
            pltpu.roll(jnp.where(index < 2, h, t), size - 2, axis),
            pltpu.roll(jnp.where(index >= size - 1, h, t), 1, axis),
            pltpu.roll(jnp.where(index >= size - 2, h, t), 2, axis),
        )

    C1, C2 = 2.0 / 3.0, 1.0 / 12.0

    def level(k, carry):
        d = dmp[k]
        d4 = 4.0 * d
        shift = 126 - 4 * k
        hx = [pltpu.roll(xh_l[i], shift, 1) for i in range(NV + 1)]
        xp1, xp2, xm1, xm2 = around(spx[k], hx[NV], lane, 128, 1)
        yp1, yp2, ym1, ym2 = around(spy[k], yh[NV, k], row, 8, 0)
        zm2, zm1, zp1, zp2 = spz[k], spz[k + 1], spz[k + 3], spz[k + 4]
        wx = ((d4 - C1 * xp1) * gx_p1, (C2 * xp2 - d) * gx_p2, (d4 + C1 * xm1) * gx_m1, (-d - C2 * xm2) * gx_m2)
        wy = ((d4 - C1 * yp1) * gy_p1, (C2 * yp2 - d) * gy_p2, (d4 + C1 * ym1) * gy_m1, (-d - C2 * ym2) * gy_m2)
        wz = (d4 - C1 * zp1, C2 * zp2 - d, d4 + C1 * zm1, -d - C2 * zm2)
        wc = -18.0 * d
        rhs = []
        for v in range(NV):
            t = st[v, k + 2]
            acc = src[v, k] + wc * t
            zs = (st[v, k + 3], st[v, k + 4], st[v, k + 1], st[v, k])
            accz = wz[0] * zs[0] + wz[1] * zs[1] + wz[2] * zs[2] + wz[3] * zs[3]
            xs = around(t, hx[v], lane, 128, 1)
            accx = wx[0] * xs[0] + wx[1] * xs[1] + wx[2] * xs[2] + wx[3] * xs[3]
            ys = around(t, yh[v, k], row, 8, 0)
            accy = wy[0] * ys[0] + wy[1] * ys[1] + wy[2] * ys[2] + wy[3] * ys[3]
            rhs.append((acc + accz) + (accx + accy))
        new = []
        for c in range(NV):
            f = left[c, 0] * rhs[0]
            for v in range(1, NV):
                f = f + left[c, v] * rhs[v]
            one_back, two_back = carry[c]
            val = f * inv_s[c, k] + far_s[c, k] * two_back - m_s[c, k] * one_back
            v_s[c, k] = val
            new.append((val, one_back))
        return tuple(new)

    ends = lax.fori_loop(0, K, level, tuple((zero, zero) for _ in range(NV)))

    def back(i, carry):
        k = K - 3 - i
        return tuple(
            (v_s[c, k] + far_s[c, k] * carry[c][1] - near_s[c, k] * carry[c][0], carry[c][0]) for c in range(NV)
        )

    firsts = lax.fori_loop(0, K - 2, back, tuple((zero, zero) for _ in range(NV)))
    for c in range(NV):
        w0, w1 = firsts[c]
        v1 = ends[c][0]
        v0 = ends[c][1] - near_s[c, K - 2] * v1
        rr_send[0, c] = de[0, c] * v0 + de[1, c] * v1
        rr_send[1, c] = de[2, c] * v0 + de[3, c] * v1
        rr_send[2, c] = de[4, c] * w0 + de[5, c] * w1
        rr_send[3, c] = de[6, c] * w0 + de[7, c] * w1
    send_all(rr_send, rr, r_send, r_recv)

    recv_all(pq, rc, c_send, c_recv)

    def block_factor(j, carry):
        p = tuple(rc[j, e] for e in range(4))
        q = tuple(rc[j + 1, 4 + e] for e in range(4))
        d = inverse(p, carry)
        t = times(d, q)
        for i, val in enumerate(d + times(d, p) + t):
            tri[j, i] = val
        return t

    lax.fori_loop(0, nnorm, block_factor, (zero, zero, zero, zero))

    recv_all(rr_send, rr, r_send, r_recv)

    def block_forward(j, carry):
        z0, z1 = carry
        r0, r1 = rr[j, 0] + rr[j + 1, 2], rr[j, 1] + rr[j + 1, 3]
        n0 = (tri[j, 0] * r0 + tri[j, 1] * r1) + (tri[j, 4] * z0 + tri[j, 5] * z1)
        n1 = (tri[j, 2] * r0 + tri[j, 3] * r1) + (tri[j, 6] * z0 + tri[j, 7] * z1)
        rr[j, 0] = n0
        rr[j, 1] = n1
        return (n0, n1)

    lax.fori_loop(0, nnorm, block_forward, (zero, zero))

    def block_back(i, carry):
        j = nnorm - 1 - i
        s0, s1 = carry
        n0 = rr[j, 0] + (tri[j, 8] * s0 + tri[j, 9] * s1)
        n1 = rr[j, 1] + (tri[j, 10] * s0 + tri[j, 11] * s1)
        sp[j + 1, 0] = n0
        sp[j + 1, 1] = n1
        return (n0, n1)

    lax.fori_loop(0, nnorm, block_back, (zero, zero))
    sp[0, 0] = zero
    sp[0, 1] = zero

    def home(t, first, count):
        return remote(
            sp.at[pl.ds(t, 2), :, 0:count, :], xsep.at[:, :, first:first + count, lax.rem(sz, 8), :],
            s_send.at[t], s_recv.at[sz], (sx, sy, t),
        )

    def home_in(t, first, count):
        return remote(
            sp.at[0:2, :, 0:count, :], xsep.at[:, :, first:first + count, lax.rem(t, 8), :],
            s_send.at[t], s_recv.at[t], (sx, sy, t),
        )

    def home_own(first, count):
        return pltpu.make_async_copy(
            sp.at[pl.ds(sz, 2), :, 0:count, :], xsep.at[:, :, first:first + count, lax.rem(sz, 8), :], s_recv.at[sz]
        )

    def home_all(first, count):
        @pl.loop(0, nnorm - 1)
        def _(i):
            home(peer(i), first, count).start()

        home_own(first, count).start()

    either(sz, home_all)

    @pl.loop(1, nnorm)
    def _(d):
        t = lax.rem(sz + d, nnorm)
        either(t, lambda first, count: home_in(t, first, count).wait_recv())

    either(sz, lambda first, count: home_own(first, count).wait())

    load[10].wait()
    own_s = [(xsep[1, 0, c], xsep[1, 1, c]) for c in range(NV)]

    def emit(k, xs):
        for v in range(NV):
            u = right[v, 0] * xs[0]
            for c in range(1, NV):
                u = u + right[v, c] * xs[c]
            out[v, k] = u

    emit(K - 1, [s[1] for s in own_s])
    emit(K - 2, [s[0] for s in own_s])

    def final(i, carry):
        k = K - 3 - i
        new = []
        for c in range(NV):
            known = v_s[c, k] + (a_s[c, k] * xsep[0, 0, c] + b_s[c, k] * xsep[0, 1, c])
            val = known + far_s[c, k] * carry[c][1] - near_s[c, k] * carry[c][0]
            new.append((val, carry[c][0]))
        emit(k, [n[0] for n in new])
        return tuple(new)

    lax.fori_loop(0, K - 2, final, tuple(own_s))

    for c in halos:
        c.wait_send()
    for c in xcopies:
        c.wait_send()
    for c in nb:
        c.wait_send()
    drain_all(pq, rc, c_send, c_recv)
    drain_all(rr_send, rr, r_send, r_recv)

    def home_drain(first, count):
        @pl.loop(1, nnorm)
        def _(d):
            home(lax.rem(sz + d, nnorm), first, count).wait_send()

    either(sz, home_drain)


def solution(mesh):
    nstream, nspan, nnorm = mesh.shape["stream"], mesh.shape["span"], mesh.shape["normal"]

    def step(state, speeds, damping, source, normal_stiff, wide_stiff, char_rates, left_vectors, right_vectors):
        K = damping.shape[0]
        T = damping.shape[1:]
        vm = lambda *s: pltpu.VMEM(s + T, F32)
        dma = lambda n: pltpu.SemaphoreType.DMA((n,))
        hbm = pl.BlockSpec(memory_space=pltpu.HBM)
        per = lambda: vm(NV, K)
        return pl.pallas_call(
            functools.partial(kernel, nstream, nspan, nnorm),
            out_shape=pltpu.VMEM(state.shape, F32),
            in_specs=[hbm] * 9,
            out_specs=pl.BlockSpec(memory_space=pltpu.VMEM),
            scratch_shapes=[
                vm(NV, K + 4), vm(K + 4), vm(K), vm(K), vm(K), vm(NV, K), vm(K), vm(K),
                vm(NV + 1, K), vm(NV + 1), vm(NV + 1), vm(NV + 1),
                per(), per(), per(), per(), per(), per(), per(),
                vm(4, NV), vm(4, NV), vm(4, NV), vm(4, NV), vm(4, NV), vm(8, NV), vm(8, NV), vm(nnorm + 1, 8),
                vm(4, NV), vm(nnorm + 1, 4), vm(nnorm, 12), vm(nnorm + 1, 2), vm(2, 2, NV), vm(2),
                pltpu.SMEM((NV,), F32), pltpu.SMEM((NV, NV), F32), pltpu.SMEM((NV, NV), F32),
                dma(11), dma(10), dma(10), dma(2), dma(2),
                dma(nnorm), dma(nnorm), dma(nnorm), dma(nnorm), dma(nnorm), dma(nnorm),
            ],
            compiler_params=pltpu.CompilerParams(
                collective_id=0, has_side_effects=True, vmem_limit_bytes=60 * 1024 * 1024
            ),
            cost_estimate=pl.CostEstimate(flops=20_000_000, bytes_accessed=2_900_000, transcendentals=0),
        )(state, speeds, damping, source, normal_stiff, wide_stiff, char_rates, left_vectors, right_vectors)

    fields = P(None, "normal", "span", "stream")
    cells = P("normal", "span", "stream")
    return jax.shard_map(
        step, mesh=mesh, in_specs=(fields, fields, cells, fields, cells, cells, P(), P(), P()),
        out_specs=fields, check_vma=False,
    )
```

```python
import functools

import jax
import jax.numpy as jnp
from jax import lax
from jax.experimental import pallas as pl
from jax.experimental.pallas import tpu as pltpu
from jax.sharding import PartitionSpec as P

MESH = pl.DeviceIdType.MESH
NV = 5
F32 = jnp.float32


def loop(begin, end, body, carry, unroll):
    def several(i, carry):
        for j in range(unroll):
            carry = body(begin + i * unroll + j, carry)
        return carry

    return lax.fori_loop(0, (end - begin) // unroll, several, carry)


def kernel(
    nstream, nspan, nnorm,
    state, speeds, damping, source, nstiff, wstiff, rates_in, left_in, right_in,
    out,
    st, spz, spy, spx, dmp, src, ns, ws,
    yh, zh_p, zh_n, xpack, xh_l, xh_r, xcor,
    inv_s, m_s, far_s, near_s, a_s, b_s, v_s,
    a_send, a_recv, n_send, n_recv, spike, de, pq, rc,
    rr_send, rr, tri, sp, xsep, consts, rates, left, right,
    load_sem, halo_send, halo_recv, nb_send, nb_recv,
    c_send, c_recv, r_send, r_recv, s_send, s_recv,
):
    K = nstiff.shape[0]
    sx = lax.axis_index("stream")
    sy = lax.axis_index("span")
    sz = lax.axis_index("normal")
    x_next, x_prev = lax.rem(sx + 1, nstream), lax.rem(sx + nstream - 1, nstream)
    y_next, y_prev = lax.rem(sy + 1, nspan), lax.rem(sy + nspan - 1, nspan)
    z_next, z_prev = lax.rem(sz + 1, nnorm), lax.rem(sz + nnorm - 1, nnorm)
    at_xn, at_xp = (x_next, sy, sz), (x_prev, sy, sz)
    at_yn, at_yp = (sx, y_next, sz), (sx, y_prev, sz)
    at_zn, at_zp = (sx, sy, z_next), (sx, sy, z_prev)

    barrier = pltpu.get_barrier_semaphore()
    def peer(i):
        return lax.rem(sz + nnorm // 2 + ((i + 1) // 2) * (1 - 2 * lax.rem(i, 2)), nnorm)

    @pl.loop(0, nnorm - 1)
    def _(i):
        pl.semaphore_signal(barrier, inc=1, device_id=(sx, sy, peer(i)), device_id_type=MESH)

    for there in (at_xn, at_xp, at_yn, at_yp):
        pl.semaphore_signal(barrier, inc=1, device_id=there, device_id_type=MESH)

    loads = [
        (rates_in, rates), (nstiff, ns), (wstiff, ws), (state, st.at[:, 2:K + 2]), (speeds.at[2], spx), (damping, dmp),
        (speeds.at[0], spz.at[2:K + 2]), (speeds.at[1], spy), (source, src), (left_in, left), (right_in, right),
    ]
    load = [pltpu.make_async_copy(a, b, load_sem.at[i]) for i, (a, b) in enumerate(loads)]
    for c in load:
        c.start()

    def remote(a, b, s, r, there):
        return pltpu.make_async_remote_copy(
            src_ref=a, dst_ref=b, send_sem=s, recv_sem=r, device_id=there, device_id_type=MESH
        )

    lane = lax.broadcasted_iota(jnp.int32, (8, 128), 1)
    row = lax.broadcasted_iota(jnp.int32, (8, 128), 0)

    load[0].wait()
    load[1].wait()
    load[2].wait()
    consts[0] = jnp.zeros((8, 128), F32)
    consts[1] = jnp.ones((8, 128), F32)
    zero, one = consts[0], consts[1]

    def factor(k, carry):
        g0, h0 = ns[k], ws[k]
        new = []
        for c in range(NV):
            near_p, far_p, a_p, b_p, near_b, far_b, a_b, b_b = carry[c]
            rate = rates[c]
            g, h = rate * g0, rate * h0
            low = h * near_b - g
            diag = (1.0 + 2.0 * (g + h)) + h * far_b - low * near_p
            inv = 1.0 / diag
            m = low * inv
            hi = h * inv
            near = (-g - low * far_p) * inv
            a = hi * a_b - m * a_p
            b = hi * b_b - m * b_p
            inv_s[c, k] = inv
            m_s[c, k] = m
            far_s[c, k] = hi
            near_s[c, k] = near
            a_s[c, k] = a
            b_s[c, k] = b
            new.append((near, -hi, a, b, near_p, far_p, a_p, b_p))
        return tuple(new)

    lax.fori_loop(0, K, factor, tuple((zero, zero, zero, one, zero, zero, one, zero) for _ in range(NV)))

    def spikes(i, carry):
        k = K - 3 - i
        new = []
        for c in range(NV):
            near, hi = near_s[c, k], far_s[c, k]
            ones = carry[c][0:4]
            twos = carry[c][4:8]
            base = (a_s[c, k], b_s[c, k], None, None)
            fresh = []
            for o, t, q in zip(ones, twos, base):
                r = hi * t - near * o
                fresh.append(r if q is None else r + q)
            new.append(tuple(fresh) + ones)
        return tuple(new)

    start = (zero, zero, one, zero, zero, zero, zero, one)
    done = lax.fori_loop(0, K - 2, spikes, tuple(start for _ in range(NV)))
    for c in range(NV):
        r0, r1 = done[c][0:4], done[c][4:8]
        for e, val in enumerate((r0[0], r0[1], r1[0], r1[1])):
            a_send[e, c] = val
        for e, val in enumerate((r0[2], r0[3], r1[2], r1[3])):
            spike[e, c] = val
        n30, n31, h30, h31 = near_s[c, K - 2], near_s[c, K - 1], far_s[c, K - 2], far_s[c, K - 1]
        for e, val in enumerate((n30 * n31 + h30, -n30 * h31, -n31, h31)):
            n_send[e, c] = val
    for k in (0, 1, K + 2, K + 3):
        spz[k] = zero
        for v in range(NV):
            st[v, k] = zero

    @pl.loop(0, K)
    def _(k):
        for v in range(NV + 1):
            yh[v, k, 2:6] = jnp.zeros((4, 128), F32)

    for e in range(4):
        rc[nnorm, 4 + e] = zero
    for e in range(2):
        rr[nnorm, 2 + e] = zero

    load[3].wait()
    load[4].wait()
    load[5].wait()
    quad = lane // 4

    def pack(k, acc):
        here = quad == k
        tiles = [st[v, k + 2] for v in range(NV)] + [spx[k], dmp[k]]
        return tuple(jnp.where(here, pltpu.roll(t, 4 * k + 2, 1), a) for t, a in zip(tiles, acc))

    packed = lax.fori_loop(0, K, pack, tuple(spx[0] for _ in range(NV + 2)))
    for i, p in enumerate(packed):
        xpack[i] = p
    pl.semaphore_wait(barrier, nnorm + 3)

    nb = [
        remote(a_send, a_recv, nb_send.at[0], nb_recv.at[0], at_zp),
        remote(n_send, n_recv, nb_send.at[1], nb_recv.at[1], at_zn),
    ]
    for c in nb:
        c.start()

    halo_list = [
        (state.at[:, :, 6:8, :], yh.at[0:NV, :, 0:2, :], at_yn),
        (state.at[:, :, 0:2, :], yh.at[0:NV, :, 6:8, :], at_yp),
        (speeds.at[1, :, 6:8, :], yh.at[NV, :, 0:2, :], at_yn),
        (speeds.at[1, :, 0:2, :], yh.at[NV, :, 6:8, :], at_yp),
        (state.at[:, K - 2:K], zh_p.at[0:NV], at_zn),
        (state.at[:, 0:2], zh_n.at[0:NV], at_zp),
        (speeds.at[0, K - 2:K], zh_p.at[NV], at_zn),
        (speeds.at[0, 0:2], zh_n.at[NV], at_zp),
    ]
    halos = [
        remote(a, b, halo_send.at[i], halo_recv.at[i], there) for i, (a, b, there) in enumerate(halo_list)
    ]
    for c in halos:
        c.start()

    xcopies = [
        remote(xpack.at[0:NV + 1], xh_l, halo_send.at[8], halo_recv.at[8], at_xn),
        remote(xpack.at[0:NV + 1], xh_r, halo_send.at[9], halo_recv.at[9], at_xp),
    ]
    for c in xcopies:
        c.start()

    for c in load[6:9]:
        c.wait()
    C1, C2 = 2.0 / 3.0, 1.0 / 12.0
    x_in = (lane < 127, lane < 126, lane > 0, lane > 1)
    y_in = (row < 7, row < 6, row > 0, row > 1)

    def around(t, size, axis):
        return tuple(pltpu.roll(t, shift, axis) for shift in (size - 1, size - 2, 1, 2))

    def interior(k, carry):
        d = dmp[k]
        d4 = 4.0 * d

        def weights(p1, p2, m1, m2):
            return d4 - C1 * p1, C2 * p2 - d, d4 + C1 * m1, -d - C2 * m2

        wx = [jnp.where(i, w, 0.0) for i, w in zip(x_in, weights(*around(spx[k], 128, 1)))]
        wy = [jnp.where(i, w, 0.0) for i, w in zip(y_in, weights(*around(spy[k], 8, 0)))]
        wz = weights(spz[k + 3], spz[k + 4], spz[k + 1], spz[k])
        wc = -18.0 * d
        for v in range(NV):
            t = st[v, k + 2]
            acc = src[v, k] + wc * t
            zs = (st[v, k + 3], st[v, k + 4], st[v, k + 1], st[v, k])
            accz = wz[0] * zs[0] + wz[1] * zs[1] + wz[2] * zs[2] + wz[3] * zs[3]
            xs = around(t, 128, 1)
            accx = wx[0] * xs[0] + wx[1] * xs[1] + wx[2] * xs[2] + wx[3] * xs[3]
            ys = around(t, 8, 0)
            accy = wy[0] * ys[0] + wy[1] * ys[1] + wy[2] * ys[2] + wy[3] * ys[3]
            src[v, k] = (acc + accz) + (accx + accy)
        return carry

    lax.fori_loop(0, K // 4, interior, 0)

    for c in nb:
        c.wait_recv()

    is_last = sz == nnorm - 1

    @pl.when(is_last)
    def _():
        for e in range(4):
            for c in range(NV):
                a_recv[e, c] = zero

    def inverse(n, a):
        m00 = 1.0 - (n[0] * a[0] + n[1] * a[2])
        m01 = -(n[0] * a[1] + n[1] * a[3])
        m10 = -(n[2] * a[0] + n[3] * a[2])
        m11 = 1.0 - (n[2] * a[1] + n[3] * a[3])
        det = 1.0 / (m00 * m11 - m01 * m10)
        return m11 * det, -m01 * det, -m10 * det, m00 * det

    def times(p, q):
        return (
            p[0] * q[0] + p[1] * q[2], p[0] * q[1] + p[1] * q[3],
            p[2] * q[0] + p[3] * q[2], p[2] * q[1] + p[3] * q[3],
        )

    for c in range(NV):
        four = lambda ref, c=c: tuple(ref[e, c] for e in range(4))
        n30, a30, a31, b30, b31 = near_s[c, K - 2], a_s[c, K - 2], a_s[c, K - 1], b_s[c, K - 2], b_s[c, K - 1]
        d = inverse(four(n_send), four(a_recv))
        p = times(d, (a30 - n30 * a31, b30 - n30 * b31, a31, b31))
        before = four(n_recv)
        e_ = times(inverse(before, four(a_send)), before)
        q = times(e_, four(spike))
        for i in range(4):
            de[i, c] = d[i]
            de[4 + i, c] = e_[i]
            pq[i, c] = p[i]
            pq[4 + i, c] = q[i]

    def heavy(t):
        return lax.rem(t, 2) == 0

    def line(t):
        return t // 2

    def either(t, do):
        pl.when(heavy(t))(lambda: do(0, 3))
        pl.when(jnp.logical_not(heavy(t)))(lambda: do(3, 2))

    def scatter(rows, land, s, r, t, first, count):
        return remote(
            rows.at[:, first:first + count, line(t), :], land.at[sz, :, 0:count, :],
            s.at[t], r.at[sz], (sx, sy, t),
        )

    def scatter_in(rows, land, s, r, t, first, count):
        return remote(
            rows.at[:, first:first + count, 0, :], land.at[t, :, 0:count, :], s.at[t], r.at[t], (sx, sy, t)
        )

    def scatter_own(rows, land, r, first, count):
        return pltpu.make_async_copy(
            rows.at[:, first:first + count, line(sz), :], land.at[sz, :, 0:count, :], r.at[sz]
        )

    def send_all(rows, land, s, r):
        @pl.loop(0, nnorm - 1)
        def _(i):
            t = peer(i)
            either(t, lambda first, count: scatter(rows, land, s, r, t, first, count).start())

        either(sz, lambda first, count: scatter_own(rows, land, r, first, count).start())

    def recv_all(rows, land, s, r):
        def every(first, count):
            @pl.loop(1, nnorm)
            def _(d):
                scatter_in(rows, land, s, r, lax.rem(sz + d, nnorm), first, count).wait_recv()

            scatter_own(rows, land, r, first, count).wait()

        either(sz, every)

    def drain_all(rows, land, s, r):
        @pl.loop(1, nnorm)
        def _(d):
            t = lax.rem(sz + d, nnorm)
            either(t, lambda first, count: scatter(rows, land, s, r, t, first, count).wait_send())

    send_all(pq, rc, c_send, c_recv)

    lax.fori_loop(K // 4, K, interior, 0)

    for c in load[9:10]:
        c.wait()
    for c in halos:
        c.wait_recv()
    for c in xcopies:
        c.wait_recv()

    @pl.when(sz > 0)
    def _():
        d0, d1, a0, a1 = dmp[0], dmp[1], zh_p[NV, 0], zh_p[NV, 1]
        w02, w01, w12 = -d0 - C2 * a0, 4.0 * d0 + C1 * a1, -d1 - C2 * a1
        for v in range(NV):
            src[v, 0] = src[v, 0] + (w02 * zh_p[v, 0] + w01 * zh_p[v, 1])
            src[v, 1] = src[v, 1] + w12 * zh_p[v, 1]

    @pl.when(sz < nnorm - 1)
    def _():
        d0, d1, a0, a1 = dmp[K - 1], dmp[K - 2], zh_n[NV, 0], zh_n[NV, 1]
        w01, w02, w12 = 4.0 * d0 - C1 * a0, C2 * a1 - d0, C2 * a0 - d1
        for v in range(NV):
            src[v, K - 1] = src[v, K - 1] + (w01 * zh_n[v, 0] + w02 * zh_n[v, 1])
            src[v, K - 2] = src[v, K - 2] + w12 * zh_n[v, 0]

    def number(yes):
        return jnp.where(yes, 1.0, 0.0).astype(F32)

    has_xn, has_xp = number(sx < nstream - 1), number(sx > 0)
    has_yn, has_yp = number(sy < nspan - 1), number(sy > 0)

    column = lax.rem(lane, 4)
    far_left, near_left = column >= 2, column == 2
    gate2 = jnp.where(far_left, has_xp, has_xn)
    sign2 = jnp.where(far_left, -C2 * has_xp, C2 * has_xn)
    near_right = column == 1
    gate1 = jnp.where(near_left, 4.0 * has_xp, jnp.where(near_right, 4.0 * has_xn, 0.0))
    sign1 = jnp.where(near_left, C1 * has_xp, jnp.where(near_right, -C1 * has_xn, 0.0))

    def columns(i):
        return (
            jnp.where(far_left, pltpu.roll(xh_l[i], 2, 1), pltpu.roll(xh_r[i], 126, 1)),
            jnp.where(near_left, pltpu.roll(xh_l[i], 1, 1), pltpu.roll(xh_r[i], 127, 1)),
        )

    a2, a1 = columns(NV)
    w2 = sign2 * a2 - gate2 * xpack[NV + 1]
    w1 = sign1 * a1 + gate1 * xpack[NV + 1]
    for v in range(NV):
        s2, s1 = columns(v)
        xcor[v] = w2 * s2 + w1 * s1
    edge = jnp.logical_or(lane < 2, lane >= 126)

    ygate2 = jnp.where(row < 2, has_yp, jnp.where(row >= 6, has_yn, 0.0))
    ysign2 = jnp.where(row < 2, -C2 * has_yp, jnp.where(row >= 6, C2 * has_yn, 0.0))
    ygate1 = jnp.where(row < 1, 4.0 * has_yp, jnp.where(row >= 7, 4.0 * has_yn, 0.0))
    ysign1 = jnp.where(row < 1, C1 * has_yp, jnp.where(row >= 7, -C1 * has_yn, 0.0))
    first = row < 1

    def nearest(h):
        return jnp.where(first, pltpu.roll(h, 7, 0), pltpu.roll(h, 1, 0))

    def level(k, carry):
        d = dmp[k]
        a2 = yh[NV, k]
        w2 = ysign2 * a2 - ygate2 * d
        w1 = ysign1 * nearest(a2) + ygate1 * d
        shift = 126 - 4 * k
        rhs = []
        for v in range(NV):
            h = yh[v, k]
            cor = jnp.where(edge, pltpu.roll(xcor[v], shift, 1), 0.0)
            rhs.append((src[v, k] + cor) + (w2 * h + w1 * nearest(h)))
        new = []
        for c in range(NV):
            f = left[c, 0] * rhs[0]
            for v in range(1, NV):
                f = f + left[c, v] * rhs[v]
            one_back, two_back = carry[c]
            val = f * inv_s[c, k] + far_s[c, k] * two_back - m_s[c, k] * one_back
            v_s[c, k] = val
            new.append((val, one_back))
        return tuple(new)

    ends = lax.fori_loop(0, K, level, tuple((zero, zero) for _ in range(NV)))

    def back(i, carry):
        k = K - 3 - i
        return tuple(
            (v_s[c, k] + far_s[c, k] * carry[c][1] - near_s[c, k] * carry[c][0], carry[c][0]) for c in range(NV)
        )

    firsts = loop(0, K - 2, back, tuple((zero, zero) for _ in range(NV)), 5)
    for c in range(NV):
        w0, w1 = firsts[c]
        v1 = ends[c][0]
        v0 = ends[c][1] - near_s[c, K - 2] * v1
        rr_send[0, c] = de[0, c] * v0 + de[1, c] * v1
        rr_send[1, c] = de[2, c] * v0 + de[3, c] * v1
        rr_send[2, c] = de[4, c] * w0 + de[5, c] * w1
        rr_send[3, c] = de[6, c] * w0 + de[7, c] * w1
    send_all(rr_send, rr, r_send, r_recv)

    recv_all(pq, rc, c_send, c_recv)

    def block_factor(j, carry):
        p = tuple(rc[j, e] for e in range(4))
        q = tuple(rc[j + 1, 4 + e] for e in range(4))
        d = inverse(p, carry)
        t = times(d, q)
        for i, val in enumerate(d + times(d, p) + t):
            tri[j, i] = val
        return t

    loop(0, nnorm, block_factor, (zero, zero, zero, zero), 4)

    recv_all(rr_send, rr, r_send, r_recv)

    def block_forward(j, carry):
        z0, z1 = carry
        r0, r1 = rr[j, 0] + rr[j + 1, 2], rr[j, 1] + rr[j + 1, 3]
        n0 = (tri[j, 0] * r0 + tri[j, 1] * r1) + (tri[j, 4] * z0 + tri[j, 5] * z1)
        n1 = (tri[j, 2] * r0 + tri[j, 3] * r1) + (tri[j, 6] * z0 + tri[j, 7] * z1)
        rr[j, 0] = n0
        rr[j, 1] = n1
        return (n0, n1)

    loop(0, nnorm, block_forward, (zero, zero), 4)

    def block_back(i, carry):
        j = nnorm - 1 - i
        s0, s1 = carry
        n0 = rr[j, 0] + (tri[j, 8] * s0 + tri[j, 9] * s1)
        n1 = rr[j, 1] + (tri[j, 10] * s0 + tri[j, 11] * s1)
        sp[j + 1, 0] = n0
        sp[j + 1, 1] = n1
        return (n0, n1)

    loop(0, nnorm, block_back, (zero, zero), 4)
    sp[0, 0] = zero
    sp[0, 1] = zero

    def home(t, first, count):
        return remote(
            sp.at[pl.ds(t, 2), :, 0:count, :], xsep.at[:, :, first:first + count, line(sz), :],
            s_send.at[t], s_recv.at[sz], (sx, sy, t),
        )

    def home_in(t, first, count):
        return remote(
            sp.at[0:2, :, 0:count, :], xsep.at[:, :, first:first + count, line(t), :],
            s_send.at[t], s_recv.at[t], (sx, sy, t),
        )

    def home_own(first, count):
        return pltpu.make_async_copy(
            sp.at[pl.ds(sz, 2), :, 0:count, :], xsep.at[:, :, first:first + count, line(sz), :], s_recv.at[sz]
        )

    def home_all(first, count):
        @pl.loop(0, nnorm - 1)
        def _(i):
            home(peer(i), first, count).start()

        home_own(first, count).start()

    either(sz, home_all)

    @pl.loop(1, nnorm)
    def _(d):
        t = lax.rem(sz + d, nnorm)
        either(t, lambda first, count: home_in(t, first, count).wait_recv())

    either(sz, lambda first, count: home_own(first, count).wait())

    load[10].wait()
    own_s = [(xsep[1, 0, c], xsep[1, 1, c]) for c in range(NV)]

    def emit(k, xs):
        for v in range(NV):
            u = right[v, 0] * xs[0]
            for c in range(1, NV):
                u = u + right[v, c] * xs[c]
            out[v, k] = u

    emit(K - 1, [s[1] for s in own_s])
    emit(K - 2, [s[0] for s in own_s])

    def final(i, carry):
        k = K - 3 - i
        new = []
        for c in range(NV):
            known = v_s[c, k] + (a_s[c, k] * xsep[0, 0, c] + b_s[c, k] * xsep[0, 1, c])
            val = known + far_s[c, k] * carry[c][1] - near_s[c, k] * carry[c][0]
            new.append((val, carry[c][0]))
        emit(k, [n[0] for n in new])
        return tuple(new)

    loop(0, K - 2, final, tuple(own_s), 1)

    for c in halos:
        c.wait_send()
    for c in xcopies:
        c.wait_send()
    for c in nb:
        c.wait_send()
    drain_all(pq, rc, c_send, c_recv)
    drain_all(rr_send, rr, r_send, r_recv)

    def home_drain(first, count):
        @pl.loop(1, nnorm)
        def _(d):
            home(lax.rem(sz + d, nnorm), first, count).wait_send()

    either(sz, home_drain)


def solution(mesh):
    nstream, nspan, nnorm = mesh.shape["stream"], mesh.shape["span"], mesh.shape["normal"]

    def step(state, speeds, damping, source, normal_stiff, wide_stiff, char_rates, left_vectors, right_vectors):
        K = damping.shape[0]
        T = damping.shape[1:]
        vm = lambda *s: pltpu.VMEM(s + T, F32)
        dma = lambda n: pltpu.SemaphoreType.DMA((n,))
        hbm = pl.BlockSpec(memory_space=pltpu.HBM)
        per = lambda: vm(NV, K)
        return pl.pallas_call(
            functools.partial(kernel, nstream, nspan, nnorm),
            out_shape=pltpu.VMEM(state.shape, F32),
            in_specs=[hbm] * 9,
            out_specs=pl.BlockSpec(memory_space=pltpu.VMEM),
            scratch_shapes=[
                vm(NV, K + 4), vm(K + 4), vm(K), vm(K), vm(K), vm(NV, K), vm(K), vm(K),
                vm(NV + 1, K), vm(NV + 1, 2), vm(NV + 1, 2), vm(NV + 2), vm(NV + 1), vm(NV + 1), vm(NV),
                per(), per(), per(), per(), per(), per(), per(),
                vm(4, NV), vm(4, NV), vm(4, NV), vm(4, NV), vm(4, NV), vm(8, NV), vm(8, NV), vm(nnorm + 1, 8),
                vm(4, NV), vm(nnorm + 1, 4), vm(nnorm, 12), vm(nnorm + 1, 2), vm(2, 2, NV), vm(2),
                pltpu.SMEM((NV,), F32), pltpu.SMEM((NV, NV), F32), pltpu.SMEM((NV, NV), F32),
                dma(11), dma(10), dma(10), dma(2), dma(2),
                dma(nnorm), dma(nnorm), dma(nnorm), dma(nnorm), dma(nnorm), dma(nnorm),
            ],
            compiler_params=pltpu.CompilerParams(
                collective_id=0, has_side_effects=True, vmem_limit_bytes=60 * 1024 * 1024
            ),
            cost_estimate=pl.CostEstimate(flops=20_000_000, bytes_accessed=2_900_000, transcendentals=0),
        )(state, speeds, damping, source, normal_stiff, wide_stiff, char_rates, left_vectors, right_vectors)

    fields = P(None, "normal", "span", "stream")
    cells = P("normal", "span", "stream")
    return jax.shard_map(
        step, mesh=mesh, in_specs=(fields, fields, cells, fields, cells, cells, P(), P(), P()),
        out_specs=fields, check_vma=False,
    )
```

```python
import functools

import jax
import jax.numpy as jnp
from jax import lax
from jax.experimental import pallas as pl
from jax.experimental.pallas import tpu as pltpu
from jax.sharding import PartitionSpec as P

MESH = pl.DeviceIdType.MESH
NV = 5
F32 = jnp.float32


def loop(begin, end, body, carry, unroll):
    def several(i, carry):
        for j in range(unroll):
            carry = body(begin + i * unroll + j, carry)
        return carry

    return lax.fori_loop(0, (end - begin) // unroll, several, carry)


def kernel(
    nstream, nspan, nnorm,
    state, speeds, damping, source, nstiff, wstiff, rates_in, left_in, right_in,
    out,
    st, spz, spy, spx, dmp, src, ns, ws,
    yh, zh_p, zh_n, xpack, xh_l, xh_r, xcor,
    inv_s, m_s, far_s, near_s, a_s, b_s, v_s,
    a_send, a_recv, n_send, n_recv, spike, de, pq, rc,
    rr_send, rr, tri, sp, xsep, consts, rates, left, right,
    load_sem, halo_send, halo_recv, nb_send, nb_recv,
    c_send, c_recv, r_send, r_recv, s_send, s_recv,
):
    K = nstiff.shape[0]
    sx = lax.axis_index("stream")
    sy = lax.axis_index("span")
    sz = lax.axis_index("normal")
    x_next, x_prev = lax.rem(sx + 1, nstream), lax.rem(sx + nstream - 1, nstream)
    y_next, y_prev = lax.rem(sy + 1, nspan), lax.rem(sy + nspan - 1, nspan)
    z_next, z_prev = lax.rem(sz + 1, nnorm), lax.rem(sz + nnorm - 1, nnorm)
    at_xn, at_xp = (x_next, sy, sz), (x_prev, sy, sz)
    at_yn, at_yp = (sx, y_next, sz), (sx, y_prev, sz)
    at_zn, at_zp = (sx, sy, z_next), (sx, sy, z_prev)

    barrier = pltpu.get_barrier_semaphore()
    def peer(i):
        return lax.rem(sz + nnorm // 2 + ((i + 1) // 2) * (1 - 2 * lax.rem(i, 2)), nnorm)

    @pl.loop(0, nnorm - 1)
    def _(i):
        pl.semaphore_signal(barrier, inc=1, device_id=(sx, sy, peer(i)), device_id_type=MESH)

    for there in (at_xn, at_xp, at_yn, at_yp):
        pl.semaphore_signal(barrier, inc=1, device_id=there, device_id_type=MESH)

    loads = [
        (rates_in, rates), (nstiff, ns), (wstiff, ws), (state, st.at[:, 2:K + 2]), (speeds.at[2], spx), (damping, dmp),
        (speeds.at[0], spz.at[2:K + 2]), (speeds.at[1], spy), (source, src), (left_in, left), (right_in, right),
    ]
    load = [pltpu.make_async_copy(a, b, load_sem.at[i]) for i, (a, b) in enumerate(loads)]
    for c in load:
        c.start()

    def remote(a, b, s, r, there):
        return pltpu.make_async_remote_copy(
            src_ref=a, dst_ref=b, send_sem=s, recv_sem=r, device_id=there, device_id_type=MESH
        )

    lane = lax.broadcasted_iota(jnp.int32, (8, 128), 1)
    row = lax.broadcasted_iota(jnp.int32, (8, 128), 0)

    load[0].wait()
    load[1].wait()
    load[2].wait()
    consts[0] = jnp.zeros((8, 128), F32)
    consts[1] = jnp.ones((8, 128), F32)
    zero, one = consts[0], consts[1]

    def factor(k, carry):
        g0, h0 = ns[k], ws[k]
        new = []
        for c in range(NV):
            near_p, far_p, a_p, b_p, near_b, far_b, a_b, b_b = carry[c]
            rate = rates[c]
            g, h = rate * g0, rate * h0
            low = h * near_b - g
            diag = (1.0 + 2.0 * (g + h)) + h * far_b - low * near_p
            inv = 1.0 / diag
            m = low * inv
            hi = h * inv
            near = (-g - low * far_p) * inv
            a = hi * a_b - m * a_p
            b = hi * b_b - m * b_p
            inv_s[c, k] = inv
            m_s[c, k] = m
            far_s[c, k] = hi
            near_s[c, k] = near
            a_s[c, k] = a
            b_s[c, k] = b
            new.append((near, -hi, a, b, near_p, far_p, a_p, b_p))
        return tuple(new)

    lax.fori_loop(0, K, factor, tuple((zero, zero, zero, one, zero, zero, one, zero) for _ in range(NV)))

    def spikes(i, carry):
        k = K - 3 - i
        new = []
        for c in range(NV):
            near, hi = near_s[c, k], far_s[c, k]
            ones = carry[c][0:4]
            twos = carry[c][4:8]
            base = (a_s[c, k], b_s[c, k], None, None)
            fresh = []
            for o, t, q in zip(ones, twos, base):
                r = hi * t - near * o
                fresh.append(r if q is None else r + q)
            new.append(tuple(fresh) + ones)
        return tuple(new)

    start = (zero, zero, one, zero, zero, zero, zero, one)
    done = lax.fori_loop(0, K - 2, spikes, tuple(start for _ in range(NV)))
    for c in range(NV):
        r0, r1 = done[c][0:4], done[c][4:8]
        for e, val in enumerate((r0[0], r0[1], r1[0], r1[1])):
            a_send[e, c] = val
        for e, val in enumerate((r0[2], r0[3], r1[2], r1[3])):
            spike[e, c] = val
        n30, n31, h30, h31 = near_s[c, K - 2], near_s[c, K - 1], far_s[c, K - 2], far_s[c, K - 1]
        for e, val in enumerate((n30 * n31 + h30, -n30 * h31, -n31, h31)):
            n_send[e, c] = val
    for k in (0, 1, K + 2, K + 3):
        spz[k] = zero
        for v in range(NV):
            st[v, k] = zero

    @pl.loop(0, K)
    def _(k):
        for v in range(NV + 1):
            yh[v, k, 2:6] = jnp.zeros((4, 128), F32)

    for e in range(4):
        rc[nnorm, 4 + e] = zero
    for e in range(2):
        rr[nnorm, 2 + e] = zero

    load[3].wait()
    load[4].wait()
    load[5].wait()
    quad = lane // 4

    def pack(k, acc):
        here = quad == k
        tiles = [st[v, k + 2] for v in range(NV)] + [spx[k], dmp[k]]
        return tuple(jnp.where(here, pltpu.roll(t, 4 * k + 2, 1), a) for t, a in zip(tiles, acc))

    packed = lax.fori_loop(0, K, pack, tuple(spx[0] for _ in range(NV + 2)))
    for i, p in enumerate(packed):
        xpack[i] = p
    pl.semaphore_wait(barrier, nnorm + 3)

    nb = [
        remote(a_send, a_recv, nb_send.at[0], nb_recv.at[0], at_zp),
        remote(n_send, n_recv, nb_send.at[1], nb_recv.at[1], at_zn),
    ]
    for c in nb:
        c.start()

    halo_list = [
        (state.at[:, :, 6:8, :], yh.at[0:NV, :, 0:2, :], at_yn),
        (state.at[:, :, 0:2, :], yh.at[0:NV, :, 6:8, :], at_yp),
        (speeds.at[1, :, 6:8, :], yh.at[NV, :, 0:2, :], at_yn),
        (speeds.at[1, :, 0:2, :], yh.at[NV, :, 6:8, :], at_yp),
        (state.at[:, K - 2:K], zh_p.at[0:NV], at_zn),
        (state.at[:, 0:2], zh_n.at[0:NV], at_zp),
        (speeds.at[0, K - 2:K], zh_p.at[NV], at_zn),
        (speeds.at[0, 0:2], zh_n.at[NV], at_zp),
    ]
    halos = [
        remote(a, b, halo_send.at[i], halo_recv.at[i], there) for i, (a, b, there) in enumerate(halo_list)
    ]
    for c in halos:
        c.start()

    xcopies = [
        remote(xpack.at[0:NV + 1], xh_l, halo_send.at[8], halo_recv.at[8], at_xn),
        remote(xpack.at[0:NV + 1], xh_r, halo_send.at[9], halo_recv.at[9], at_xp),
    ]
    for c in xcopies:
        c.start()

    for c in load[6:9]:
        c.wait()
    C1, C2 = 2.0 / 3.0, 1.0 / 12.0
    x_in = (lane < 127, lane < 126, lane > 0, lane > 1)
    y_in = (row < 7, row < 6, row > 0, row > 1)

    def around(t, size, axis):
        return tuple(pltpu.roll(t, shift, axis) for shift in (size - 1, size - 2, 1, 2))

    def interior(k, carry):
        d = dmp[k]
        d4 = 4.0 * d

        def weights(p1, p2, m1, m2):
            return d4 - C1 * p1, C2 * p2 - d, d4 + C1 * m1, -d - C2 * m2

        wx = [jnp.where(i, w, 0.0) for i, w in zip(x_in, weights(*around(spx[k], 128, 1)))]
        wy = [jnp.where(i, w, 0.0) for i, w in zip(y_in, weights(*around(spy[k], 8, 0)))]
        wz = weights(spz[k + 3], spz[k + 4], spz[k + 1], spz[k])
        wc = -18.0 * d
        for v in range(NV):
            t = st[v, k + 2]
            acc = src[v, k] + wc * t
            zs = (st[v, k + 3], st[v, k + 4], st[v, k + 1], st[v, k])
            accz = wz[0] * zs[0] + wz[1] * zs[1] + wz[2] * zs[2] + wz[3] * zs[3]
            xs = around(t, 128, 1)
            accx = wx[0] * xs[0] + wx[1] * xs[1] + wx[2] * xs[2] + wx[3] * xs[3]
            ys = around(t, 8, 0)
            accy = wy[0] * ys[0] + wy[1] * ys[1] + wy[2] * ys[2] + wy[3] * ys[3]
            src[v, k] = (acc + accz) + (accx + accy)
        return carry

    lax.fori_loop(0, K // 4, interior, 0)

    for c in nb:
        c.wait_recv()

    is_last = sz == nnorm - 1

    @pl.when(is_last)
    def _():
        for e in range(4):
            for c in range(NV):
                a_recv[e, c] = zero

    def inverse(n, a):
        m00 = 1.0 - (n[0] * a[0] + n[1] * a[2])
        m01 = -(n[0] * a[1] + n[1] * a[3])
        m10 = -(n[2] * a[0] + n[3] * a[2])
        m11 = 1.0 - (n[2] * a[1] + n[3] * a[3])
        det = 1.0 / (m00 * m11 - m01 * m10)
        return m11 * det, -m01 * det, -m10 * det, m00 * det

    def times(p, q):
        return (
            p[0] * q[0] + p[1] * q[2], p[0] * q[1] + p[1] * q[3],
            p[2] * q[0] + p[3] * q[2], p[2] * q[1] + p[3] * q[3],
        )

    def heavy(t):
        return lax.rem(t, 2) == 0

    def line(t):
        return t // 2

    def either(t, do):
        pl.when(heavy(t))(lambda: do(0, 3))
        pl.when(jnp.logical_not(heavy(t)))(lambda: do(3, 2))

    def scatter(rows, land, s, r, t, first, count):
        return remote(
            rows.at[:, first:first + count, line(t), :], land.at[sz, :, 0:count, :],
            s.at[t], r.at[sz], (sx, sy, t),
        )

    def scatter_in(rows, land, s, r, t, first, count):
        return remote(
            rows.at[:, first:first + count, 0, :], land.at[t, :, 0:count, :], s.at[t], r.at[t], (sx, sy, t)
        )

    def scatter_own(rows, land, r, first, count):
        return pltpu.make_async_copy(
            rows.at[:, first:first + count, line(sz), :], land.at[sz, :, 0:count, :], r.at[sz]
        )

    def send_all(rows, land, s, r):
        @pl.loop(0, nnorm - 1)
        def _(i):
            t = peer(i)
            either(t, lambda first, count: scatter(rows, land, s, r, t, first, count).start())

        either(sz, lambda first, count: scatter_own(rows, land, r, first, count).start())

    def recv_all(rows, land, s, r):
        def every(first, count):
            @pl.loop(1, nnorm)
            def _(d):
                scatter_in(rows, land, s, r, lax.rem(sz + d, nnorm), first, count).wait_recv()

            scatter_own(rows, land, r, first, count).wait()

        either(sz, every)

    def drain_all(rows, land, s, r):
        @pl.loop(1, nnorm)
        def _(d):
            t = lax.rem(sz + d, nnorm)
            either(t, lambda first, count: scatter(rows, land, s, r, t, first, count).wait_send())

    def blocks(c):
        four = lambda ref: tuple(ref[e, c] for e in range(4))
        n30, a30, a31, b30, b31 = near_s[c, K - 2], a_s[c, K - 2], a_s[c, K - 1], b_s[c, K - 2], b_s[c, K - 1]
        d = inverse(four(n_send), four(a_recv))
        p = times(d, (a30 - n30 * a31, b30 - n30 * b31, a31, b31))
        before = four(n_recv)
        e_ = times(inverse(before, four(a_send)), before)
        q = times(e_, four(spike))
        for i in range(4):
            de[i, c] = d[i]
            de[4 + i, c] = e_[i]
            pq[i, c] = p[i]
            pq[4 + i, c] = q[i]

    for first, count in ((3, 2), (0, 3)):
        for c in range(first, first + count):
            blocks(c)

        @pl.loop(0, nnorm - 1)
        def _(i):
            t = peer(i)

            @pl.when(heavy(t) if count == 3 else jnp.logical_not(heavy(t)))
            def _():
                scatter(pq, rc, c_send, c_recv, t, first, count).start()

    either(sz, lambda first, count: scatter_own(pq, rc, c_recv, first, count).start())

    lax.fori_loop(K // 4, K, interior, 0)

    for c in load[9:10]:
        c.wait()
    for c in halos:
        c.wait_recv()
    for c in xcopies:
        c.wait_recv()

    @pl.when(sz > 0)
    def _():
        d0, d1, a0, a1 = dmp[0], dmp[1], zh_p[NV, 0], zh_p[NV, 1]
        w02, w01, w12 = -d0 - C2 * a0, 4.0 * d0 + C1 * a1, -d1 - C2 * a1
        for v in range(NV):
            src[v, 0] = src[v, 0] + (w02 * zh_p[v, 0] + w01 * zh_p[v, 1])
            src[v, 1] = src[v, 1] + w12 * zh_p[v, 1]

    @pl.when(sz < nnorm - 1)
    def _():
        d0, d1, a0, a1 = dmp[K - 1], dmp[K - 2], zh_n[NV, 0], zh_n[NV, 1]
        w01, w02, w12 = 4.0 * d0 - C1 * a0, C2 * a1 - d0, C2 * a0 - d1
        for v in range(NV):
            src[v, K - 1] = src[v, K - 1] + (w01 * zh_n[v, 0] + w02 * zh_n[v, 1])
            src[v, K - 2] = src[v, K - 2] + w12 * zh_n[v, 0]

    def number(yes):
        return jnp.where(yes, 1.0, 0.0).astype(F32)

    has_xn, has_xp = number(sx < nstream - 1), number(sx > 0)
    has_yn, has_yp = number(sy < nspan - 1), number(sy > 0)

    column = lax.rem(lane, 4)
    far_left, near_left = column >= 2, column == 2
    gate2 = jnp.where(far_left, has_xp, has_xn)
    sign2 = jnp.where(far_left, -C2 * has_xp, C2 * has_xn)
    near_right = column == 1
    gate1 = jnp.where(near_left, 4.0 * has_xp, jnp.where(near_right, 4.0 * has_xn, 0.0))
    sign1 = jnp.where(near_left, C1 * has_xp, jnp.where(near_right, -C1 * has_xn, 0.0))

    def columns(i):
        return (
            jnp.where(far_left, pltpu.roll(xh_l[i], 2, 1), pltpu.roll(xh_r[i], 126, 1)),
            jnp.where(near_left, pltpu.roll(xh_l[i], 1, 1), pltpu.roll(xh_r[i], 127, 1)),
        )

    a2, a1 = columns(NV)
    w2 = sign2 * a2 - gate2 * xpack[NV + 1]
    w1 = sign1 * a1 + gate1 * xpack[NV + 1]
    for v in range(NV):
        s2, s1 = columns(v)
        xcor[v] = w2 * s2 + w1 * s1
    edge = jnp.logical_or(lane < 2, lane >= 126)

    ygate2 = jnp.where(row < 2, has_yp, jnp.where(row >= 6, has_yn, 0.0))
    ysign2 = jnp.where(row < 2, -C2 * has_yp, jnp.where(row >= 6, C2 * has_yn, 0.0))
    ygate1 = jnp.where(row < 1, 4.0 * has_yp, jnp.where(row >= 7, 4.0 * has_yn, 0.0))
    ysign1 = jnp.where(row < 1, C1 * has_yp, jnp.where(row >= 7, -C1 * has_yn, 0.0))
    first = row < 1

    def nearest(h):
        return jnp.where(first, pltpu.roll(h, 7, 0), pltpu.roll(h, 1, 0))

    def level(k, carry):
        d = dmp[k]
        a2 = yh[NV, k]
        w2 = ysign2 * a2 - ygate2 * d
        w1 = ysign1 * nearest(a2) + ygate1 * d
        shift = 126 - 4 * k
        rhs = []
        for v in range(NV):
            h = yh[v, k]
            cor = jnp.where(edge, pltpu.roll(xcor[v], shift, 1), 0.0)
            rhs.append((src[v, k] + cor) + (w2 * h + w1 * nearest(h)))
        new = []
        for c in range(NV):
            f = left[c, 0] * rhs[0]
            for v in range(1, NV):
                f = f + left[c, v] * rhs[v]
            one_back, two_back = carry[c]
            val = f * inv_s[c, k] + far_s[c, k] * two_back - m_s[c, k] * one_back
            v_s[c, k] = val
            new.append((val, one_back))
        return tuple(new)

    ends = lax.fori_loop(0, K, level, tuple((zero, zero) for _ in range(NV)))

    def back(i, carry):
        k = K - 3 - i
        return tuple(
            (v_s[c, k] + far_s[c, k] * carry[c][1] - near_s[c, k] * carry[c][0], carry[c][0]) for c in range(NV)
        )

    firsts = loop(0, K - 2, back, tuple((zero, zero) for _ in range(NV)), 5)
    for c in range(NV):
        w0, w1 = firsts[c]
        v1 = ends[c][0]
        v0 = ends[c][1] - near_s[c, K - 2] * v1
        rr_send[0, c] = de[0, c] * v0 + de[1, c] * v1
        rr_send[1, c] = de[2, c] * v0 + de[3, c] * v1
        rr_send[2, c] = de[4, c] * w0 + de[5, c] * w1
        rr_send[3, c] = de[6, c] * w0 + de[7, c] * w1
    send_all(rr_send, rr, r_send, r_recv)

    recv_all(pq, rc, c_send, c_recv)

    def block_factor(j, carry):
        p = tuple(rc[j, e] for e in range(4))
        q = tuple(rc[j + 1, 4 + e] for e in range(4))
        d = inverse(p, carry)
        t = times(d, q)
        for i, val in enumerate(d + times(d, p) + t):
            tri[j, i] = val
        return t

    loop(0, nnorm, block_factor, (zero, zero, zero, zero), 4)

    recv_all(rr_send, rr, r_send, r_recv)

    def block_forward(j, carry):
        z0, z1 = carry
        r0, r1 = rr[j, 0] + rr[j + 1, 2], rr[j, 1] + rr[j + 1, 3]
        n0 = (tri[j, 0] * r0 + tri[j, 1] * r1) + (tri[j, 4] * z0 + tri[j, 5] * z1)
        n1 = (tri[j, 2] * r0 + tri[j, 3] * r1) + (tri[j, 6] * z0 + tri[j, 7] * z1)
        rr[j, 0] = n0
        rr[j, 1] = n1
        return (n0, n1)

    loop(0, nnorm, block_forward, (zero, zero), 4)

    def block_back(i, carry):
        j = nnorm - 1 - i
        s0, s1 = carry
        n0 = rr[j, 0] + (tri[j, 8] * s0 + tri[j, 9] * s1)
        n1 = rr[j, 1] + (tri[j, 10] * s0 + tri[j, 11] * s1)
        sp[j + 1, 0] = n0
        sp[j + 1, 1] = n1
        return (n0, n1)

    loop(0, nnorm, block_back, (zero, zero), 4)
    sp[0, 0] = zero
    sp[0, 1] = zero

    def home(t, first, count):
        return remote(
            sp.at[pl.ds(t, 2), :, 0:count, :], xsep.at[:, :, first:first + count, line(sz), :],
            s_send.at[t], s_recv.at[sz], (sx, sy, t),
        )

    def home_in(t, first, count):
        return remote(
            sp.at[0:2, :, 0:count, :], xsep.at[:, :, first:first + count, line(t), :],
            s_send.at[t], s_recv.at[t], (sx, sy, t),
        )

    def home_own(first, count):
        return pltpu.make_async_copy(
            sp.at[pl.ds(sz, 2), :, 0:count, :], xsep.at[:, :, first:first + count, line(sz), :], s_recv.at[sz]
        )

    def home_all(first, count):
        @pl.loop(0, nnorm - 1)
        def _(i):
            home(peer(i), first, count).start()

        home_own(first, count).start()

    either(sz, home_all)

    @pl.loop(1, nnorm)
    def _(d):
        t = lax.rem(sz + d, nnorm)
        either(t, lambda first, count: home_in(t, first, count).wait_recv())

    either(sz, lambda first, count: home_own(first, count).wait())

    load[10].wait()
    own_s = [(xsep[1, 0, c], xsep[1, 1, c]) for c in range(NV)]

    def emit(k, xs):
        for v in range(NV):
            u = right[v, 0] * xs[0]
            for c in range(1, NV):
                u = u + right[v, c] * xs[c]
            out[v, k] = u

    emit(K - 1, [s[1] for s in own_s])
    emit(K - 2, [s[0] for s in own_s])

    def final(i, carry):
        k = K - 3 - i
        new = []
        for c in range(NV):
            known = v_s[c, k] + (a_s[c, k] * xsep[0, 0, c] + b_s[c, k] * xsep[0, 1, c])
            val = known + far_s[c, k] * carry[c][1] - near_s[c, k] * carry[c][0]
            new.append((val, carry[c][0]))
        emit(k, [n[0] for n in new])
        return tuple(new)

    loop(0, K - 2, final, tuple(own_s), 1)

    for c in halos:
        c.wait_send()
    for c in xcopies:
        c.wait_send()
    for c in nb:
        c.wait_send()
    drain_all(pq, rc, c_send, c_recv)
    drain_all(rr_send, rr, r_send, r_recv)

    def home_drain(first, count):
        @pl.loop(1, nnorm)
        def _(d):
            home(lax.rem(sz + d, nnorm), first, count).wait_send()

    either(sz, home_drain)


def solution(mesh):
    nstream, nspan, nnorm = mesh.shape["stream"], mesh.shape["span"], mesh.shape["normal"]

    def step(state, speeds, damping, source, normal_stiff, wide_stiff, char_rates, left_vectors, right_vectors):
        K = damping.shape[0]
        T = damping.shape[1:]
        vm = lambda *s: pltpu.VMEM(s + T, F32)
        dma = lambda n: pltpu.SemaphoreType.DMA((n,))
        hbm = pl.BlockSpec(memory_space=pltpu.HBM)
        per = lambda: vm(NV, K)
        return pl.pallas_call(
            functools.partial(kernel, nstream, nspan, nnorm),
            out_shape=pltpu.VMEM(state.shape, F32),
            in_specs=[hbm] * 9,
            out_specs=pl.BlockSpec(memory_space=pltpu.VMEM),
            scratch_shapes=[
                vm(NV, K + 4), vm(K + 4), vm(K), vm(K), vm(K), vm(NV, K), vm(K), vm(K),
                vm(NV + 1, K), vm(NV + 1, 2), vm(NV + 1, 2), vm(NV + 2), vm(NV + 1), vm(NV + 1), vm(NV),
                per(), per(), per(), per(), per(), per(), per(),
                vm(4, NV), vm(4, NV), vm(4, NV), vm(4, NV), vm(4, NV), vm(8, NV), vm(8, NV), vm(nnorm + 1, 8),
                vm(4, NV), vm(nnorm + 1, 4), vm(nnorm, 12), vm(nnorm + 1, 2), vm(2, 2, NV), vm(2),
                pltpu.SMEM((NV,), F32), pltpu.SMEM((NV, NV), F32), pltpu.SMEM((NV, NV), F32),
                dma(11), dma(10), dma(10), dma(2), dma(2),
                dma(nnorm), dma(nnorm), dma(nnorm), dma(nnorm), dma(nnorm), dma(nnorm),
            ],
            compiler_params=pltpu.CompilerParams(
                collective_id=0, has_side_effects=True, vmem_limit_bytes=60 * 1024 * 1024
            ),
            cost_estimate=pl.CostEstimate(flops=20_000_000, bytes_accessed=2_900_000, transcendentals=0),
        )(state, speeds, damping, source, normal_stiff, wide_stiff, char_rates, left_vectors, right_vectors)

    fields = P(None, "normal", "span", "stream")
    cells = P("normal", "span", "stream")
    return jax.shard_map(
        step, mesh=mesh, in_specs=(fields, fields, cells, fields, cells, cells, P(), P(), P()),
        out_specs=fields, check_vma=False,
    )
```
